128 devices in a mesh: row: 16 (over y, z), col: 8 (over x, core).
Axes of the slice: x: 4, y: 4, z: 4, core: 2. Of those that a mesh axis runs over, the one named last changes fastest.
Arguments:
- object_real: float32 [8192, 4096], P('row', 'col'), may hold values from -5 to 5
- object_imag: float32 [8192, 4096], P('row', 'col'), may hold values from -5 to 5
- probe_real: float32 [4, 256, 256], replicated, may hold values from -6 to 6
- probe_imag: float32 [4, 256, 256], replicated, may hold values from -6 to 6
- amplitudes: float32 [16, 8, 8, 256, 256], P('row', 'col'), may hold values from 0 to 3
- positions: int32 [16, 8, 8, 2], P('row', 'col'), may hold values from 0 to 511, as said below
- counts: int32 [16, 8], P('row', 'col'), may hold values from 1 to 8, as said below
Outputs:
- new_object_real: float32 [8192, 4096], P('row', 'col')
- new_object_imag: float32 [8192, 4096], P('row', 'col')
- new_probe_real: float32 [4, 256, 256], replicated
- new_probe_imag: float32 [4, 256, 256], replicated
The draws below stay inside these ranges and needn't reach their ends.
Inputs may be any that keep to these rules, and one draw needn't show every extreme that they name: `positions`: offsets lie within the device's tile; on the last row of devices the row offset is at most 256, on the last column the column offset likewise, so every frame's window lies inside the object. `counts`: slots from the count on hold no frame.
All inputs are finite; a program needn't handle non-finite values.
Results may differ from the reference program's by a relative error of at most 0.0046.
Values sent between devices are 32-bit elements; how exact they have to be, the bound alone decides.
A program may use at most 128 MiB of HBM per device.

```python
import math
import jax
import jax.numpy as jnp
from jax import lax

P_SIZE = 256
M = 4
TILE = 512
FR_CAP = 8
NY = 8192
NX = 4096
N_ROW = 16
N_COL = 8


def draw_positions(key, part):
    key = jax.random.fold_in(key, 3)
    keys = jax.random.split(key, 4)
    rows = jnp.arange(N_ROW, dtype=jnp.int32)[:, None, None]
    cols = jnp.arange(N_COL, dtype=jnp.int32)[None, :, None]
    shape = (N_ROW, N_COL, FR_CAP)
    limit_y = jnp.broadcast_to(jnp.where(rows == N_ROW - 1, TILE - P_SIZE + 1, TILE), shape)
    limit_x = jnp.broadcast_to(jnp.where(cols == N_COL - 1, TILE - P_SIZE + 1, TILE), shape)
    offset_y = jax.random.randint(keys[0], shape, 0, limit_y)
    offset_x = jax.random.randint(keys[1], shape, 0, limit_x)
    pick_r = jax.random.randint(keys[2], (), 0, N_ROW - 1)
    pick_c = jax.random.randint(keys[3], (), 0, N_COL - 1)
    offset_y = offset_y.at[pick_r, pick_c, 0].set(TILE - 1).at[pick_r, pick_c, 1].set(0)
    offset_x = offset_x.at[pick_r, pick_c, 0].set(TILE - 1).at[pick_r, pick_c, 1].set(0)
    return jnp.stack([offset_y, offset_x], axis=-1).astype(jnp.int32)


def draw_counts(key, part):
    key = jax.random.fold_in(key, 5)
    keys = jax.random.split(key, 3)
    number = N_ROW * N_COL
    values = jax.random.randint(keys[0], (number,), 1, FR_CAP + 1)
    first = jax.random.randint(keys[1], (), 0, number)
    second = (first + 1 + jax.random.randint(keys[2], (), 0, number - 1)) % number
    values = values.at[first].set(FR_CAP).at[second].set(1)
    return values.reshape(N_ROW, N_COL).astype(jnp.int32)


def levels(own_key, dims, cuts, smallest, high):
    def one(axis_at, parts):
        draws = jax.random.uniform(jax.random.fold_in(jax.random.fold_in(own_key, 6), axis_at), (parts,), jnp.float32, smallest / len(cuts), high / len(cuts))
        return jnp.repeat(jnp.exp(draws), dims[axis_at] // parts).reshape((-1,) + (1,) * (len(dims) - axis_at - 1))

    loudness = one(*cuts[0])
    for cut in cuts[1:]:
        loudness = loudness * one(*cut)
    return loudness


def normal_values(key, shape, spread, most, cuts=(), kind=jnp.bfloat16):
    gain = levels(key, shape, cuts, -0.22, 0.18) if cuts else 1.0
    array = jax.random.normal(key, shape, jnp.float32) * spread * gain
    return jnp.minimum(jnp.maximum(array, -most), most).astype(kind)


def setup_inputs(seed: int = 0) -> dict:
    arg_keys = jax.random.split(jax.random.key(seed), 8)
    return {
        "object_real": normal_values(arg_keys[0], (NY, NX), 0.7, 5.0, ((0, 16), (1, 8)), jnp.float32),
        "object_imag": normal_values(arg_keys[1], (NY, NX), 0.7, 5.0, ((0, 16), (1, 8)), jnp.float32),
        "probe_real": normal_values(arg_keys[2], (M, P_SIZE, P_SIZE), 1.0, 6.0, (), jnp.float32),
        "probe_imag": normal_values(arg_keys[3], (M, P_SIZE, P_SIZE), 1.0, 6.0, (), jnp.float32),
        "amplitudes": jnp.clip(3.0 * jax.random.uniform(arg_keys[4], (N_ROW, N_COL, FR_CAP, P_SIZE, P_SIZE), jnp.float32) ** levels(arg_keys[4], (N_ROW, N_COL, FR_CAP, P_SIZE, P_SIZE), ((0, 16), (1, 8)), -0.2, 0.2), 0.0, 3.0),
        "positions": draw_positions(jax.random.fold_in(arg_keys[7], 71), 0),
        "counts": draw_counts(jax.random.fold_in(arg_keys[7], 71), 0),
    }


OBJECT_STEP = 0.25
PROBE_STEP = 0.5

def dft_tables(length):
    index = jnp.arange(length, dtype=jnp.int32)
    phase = index[:, None] * index[None, :] % length
    angle = phase.astype(jnp.float32) * (2.0 * math.pi / length)
    scale = 1.0 / math.sqrt(length)
    return ((jnp.cos(angle) * scale).astype(jnp.bfloat16), (-jnp.sin(angle) * scale).astype(jnp.bfloat16))

def left_product(table, field):
    return jnp.einsum('jk,mkl->mjl', table.astype(jnp.float32), field.astype(jnp.float32))

def right_product(field, table):
    return jnp.einsum('mjk,kl->mjl', field.astype(jnp.float32), table.astype(jnp.float32))

def frame_gradient(patch_r, patch_i, amp, probe_r, probe_i, cos_t, sin_t):
    wave_r = (probe_r * patch_r - probe_i * patch_i).astype(jnp.bfloat16)
    wave_i = (probe_r * patch_i + probe_i * patch_r).astype(jnp.bfloat16)
    half_r = (left_product(cos_t, wave_r) - left_product(sin_t, wave_i)).astype(jnp.bfloat16)
    half_i = (left_product(cos_t, wave_i) + left_product(sin_t, wave_r)).astype(jnp.bfloat16)
    far_r = right_product(half_r, cos_t) - right_product(half_i, sin_t)
    far_i = right_product(half_r, sin_t) + right_product(half_i, cos_t)
    intensity = lax.optimization_barrier(jnp.sum(far_r * far_r + far_i * far_i, axis=0))
    factor = 1.0 - amp / jnp.maximum(jnp.sqrt(intensity), 0.5)
    chi_r = (far_r * factor).astype(jnp.bfloat16)
    chi_i = (far_i * factor).astype(jnp.bfloat16)
    back_r = (left_product(cos_t, chi_r) + left_product(sin_t, chi_i)).astype(jnp.bfloat16)
    back_i = (left_product(cos_t, chi_i) - left_product(sin_t, chi_r)).astype(jnp.bfloat16)
    grad_r = right_product(back_r, cos_t) + right_product(back_i, sin_t)
    grad_i = right_product(back_i, cos_t) - right_product(back_r, sin_t)
    obj_r = lax.optimization_barrier(jnp.sum(probe_r * grad_r + probe_i * grad_i, axis=0))
    obj_i = lax.optimization_barrier(jnp.sum(probe_r * grad_i - probe_i * grad_r, axis=0))
    prb_r = patch_r * grad_r + patch_i * grad_i
    prb_i = patch_r * grad_i - patch_i * grad_r
    return (obj_r, obj_i, prb_r, prb_i)

def reference(object_real, object_imag, probe_real, probe_imag, amplitudes, positions, counts):
    cos_t, sin_t = dft_tables(P_SIZE)
    total = N_ROW * N_COL * FR_CAP

    def step(carry, index):
        grad_r, grad_i, pgrad_r, pgrad_i = carry
        dev_r = index // (N_COL * FR_CAP)
        dev_c = index // FR_CAP % N_COL
        slot = index % FR_CAP
        top = (dev_r * TILE + positions[dev_r, dev_c, slot, 0]).astype(jnp.int32)
        left = (dev_c * TILE + positions[dev_r, dev_c, slot, 1]).astype(jnp.int32)
        live = slot < counts[dev_r, dev_c]

        def work(unused):
            patch_r = lax.dynamic_slice(object_real, (top, left), (P_SIZE, P_SIZE))
            patch_i = lax.dynamic_slice(object_imag, (top, left), (P_SIZE, P_SIZE))
            return frame_gradient(patch_r, patch_i, amplitudes[dev_r, dev_c, slot], probe_real, probe_imag, cos_t, sin_t)

        def empty(unused):
            zero_obj = jnp.zeros((P_SIZE, P_SIZE), jnp.float32)
            zero_prb = jnp.zeros((M, P_SIZE, P_SIZE), jnp.float32)
            return (zero_obj, zero_obj, zero_prb, zero_prb)
        obj_r, obj_i, prb_r, prb_i = lax.cond(live, work, empty, 0)
        old_r = lax.dynamic_slice(grad_r, (top, left), (P_SIZE, P_SIZE))
        old_i = lax.dynamic_slice(grad_i, (top, left), (P_SIZE, P_SIZE))
        grad_r = lax.dynamic_update_slice(grad_r, old_r + obj_r, (top, left))
        grad_i = lax.dynamic_update_slice(grad_i, old_i + obj_i, (top, left))
        return ((grad_r, grad_i, pgrad_r + prb_r, pgrad_i + prb_i), None)
    init = (jnp.zeros((NY, NX), jnp.float32), jnp.zeros((NY, NX), jnp.float32), jnp.zeros((M, P_SIZE, P_SIZE), jnp.float32), jnp.zeros((M, P_SIZE, P_SIZE), jnp.float32))
    carry, unused = lax.scan(step, init, jnp.arange(total, dtype=jnp.int32))
    grad_r, grad_i, pgrad_r, pgrad_i = carry
    probe_step = PROBE_STEP / math.sqrt(FR_CAP * N_ROW * N_COL)
    return (object_real - OBJECT_STEP * grad_r, object_imag - OBJECT_STEP * grad_i, probe_real - probe_step * pgrad_r, probe_imag - probe_step * pgrad_i)
```

```python
import math

import jax
import jax.numpy as jnp
import numpy as np
from jax import lax
from jax.experimental import pallas as pl
from jax.experimental.pallas import tpu as pltpu
from jax.sharding import PartitionSpec as P

OBJECT_STEP = 0.25
PROBE_STEP = 0.5
MESH = pl.DeviceIdType.MESH
F32 = jnp.float32
BF16 = jnp.bfloat16
LANES = 128
SIZE = 256
MODES = 4
TILE = 512
SPAN = TILE + SIZE
SLOTS = 8
CHUNK = 32
VMEM_LIMIT = 56 * 2**20


def tables():
    index = np.arange(SIZE)
    angle = (index[:, None] * index[None, :] % SIZE) * (2.0 * math.pi / SIZE)
    scale = 1.0 / math.sqrt(SIZE)
    cos_t = (np.cos(angle) * scale).astype(BF16)
    sin_t = (-np.sin(angle) * scale).astype(BF16)
    found = []
    for parity in range(2):
        c = cos_t[parity::2, : SIZE // 2]
        s = sin_t[parity::2, : SIZE // 2]
        table = np.block([[c, -s], [s, c]])
        found += [table, np.ascontiguousarray(table.T)]
    return np.stack(found)


def parity_order():
    order = np.concatenate([np.arange(0, SIZE, 2), np.arange(1, SIZE, 2)])
    right = np.arange(SIZE)[:, None] == order[None, :]
    return np.stack([right, right.T]).astype(BF16)


def dot(a, b):
    return jnp.dot(a, b, preferred_element_type=F32)


def grid_place():
    return lax.axis_index("row"), lax.axis_index("col")


def greet(peers):
    barrier = pltpu.get_barrier_semaphore()
    for peer in peers:
        pl.semaphore_signal(barrier, inc=1, device_id=peer, device_id_type=MESH)
    pl.semaphore_wait(barrier, len(peers))


def halo_kernel(rows, cols, obj_r, obj_i, amp, order, ext, amp_out, own_sem, send_sem, recv_sem):
    row, col = grid_place()
    up = (lax.rem(row + rows - 1, rows), col)
    down = (lax.rem(row + 1, rows), col)
    left = (row, lax.rem(col + cols - 1, cols))
    right = (row, lax.rem(col + 1, cols))
    greet((up, down, left, right))
    objs = (obj_r, obj_i)

    def band(part, j, number):
        return pltpu.make_async_remote_copy(
            src_ref=objs[part].at[pl.ds(0, SIZE), pl.ds(j * LANES, LANES)],
            dst_ref=ext.at[part, j, pl.ds(TILE, SIZE), :],
            send_sem=send_sem.at[number],
            recv_sem=recv_sem.at[number],
            device_id=up,
            device_id_type=MESH,
        )

    def side(part, j, number):
        return pltpu.make_async_remote_copy(
            src_ref=objs[part].at[:, pl.ds(j * LANES, LANES)],
            dst_ref=ext.at[part, 4 + j, pl.ds(0, TILE), :],
            send_sem=send_sem.at[number],
            recv_sem=recv_sem.at[number],
            device_id=left,
            device_id_type=MESH,
        )

    def corner(part, j, number):
        return pltpu.make_async_remote_copy(
            src_ref=ext.at[part, j, pl.ds(TILE, SIZE), :],
            dst_ref=ext.at[part, 4 + j, pl.ds(TILE, SIZE), :],
            send_sem=send_sem.at[number],
            recv_sem=recv_sem.at[number],
            device_id=left,
            device_id_type=MESH,
        )

    bands = [band(part, j, 2 * j + part) for j in range(4) for part in range(2)]
    sides = [side(part, j, 8 + 2 * j + part) for j in range(2) for part in range(2)]
    corners = [corner(part, j, 12 + 2 * j + part) for j in range(2) for part in range(2)]
    own = [
        pltpu.make_async_copy(
            objs[part].at[:, pl.ds(j * LANES, LANES)],
            ext.at[part, j, pl.ds(0, TILE), :],
            own_sem.at[2 * j + part],
        )
        for j in range(4)
        for part in range(2)
    ]
    for copy in bands + sides + own:
        copy.start()

    def sort(slot, carry):
        a = amp[slot]
        by_row = jnp.zeros((SIZE, SIZE), F32)
        for step in range(3):
            piece = a.astype(BF16)
            by_row += dot(order[1], piece)
            a = a - piece.astype(F32)
        total = jnp.zeros((SIZE, SIZE), F32)
        for step in range(3):
            piece = by_row.astype(BF16)
            total += dot(piece, order[0])
            by_row = by_row - piece.astype(F32)
        amp_out[slot] = total
        return carry

    lax.fori_loop(0, SLOTS, sort, 0)
    for number in range(4):
        bands[number].wait_recv()
        corners[number].start()
    for copy in own:
        copy.wait()
    for copy in bands:
        copy.wait_send()
    for copy in bands[4:]:
        copy.wait_recv()
    for copy in sides + corners:
        copy.wait()


def frames_kernel(
    pos, cnt, ext, amp, pr, pi, tab, acc, pg, pat_r, pat_i, xp, xq, far_e, far_o, inten, og_r, og_i
):
    half = SIZE // 2
    blank = jnp.zeros((SPAN, LANES), F32)
    for part in range(2):
        for j in range(6):
            acc[part, j] = blank
        for m in range(MODES):
            pg[part, m] = jnp.zeros((SIZE, SIZE), F32)

    def frame(s, carry):
        y = pos[2 * s]
        x = pos[2 * s + 1]
        jb = x // LANES
        sh = x % LANES
        back = (LANES - sh) % LANES
        lane = lax.broadcasted_iota(jnp.int32, (CHUNK, LANES), 1)
        keep = lane < LANES - sh
        for part, dst in ((0, pat_r), (1, pat_i)):
            for c in range(0, SIZE, CHUNK):
                a, b, d = (
                    pltpu.roll(ext[part, jb + t, pl.ds(y + c, CHUNK), :], back, 1) for t in range(3)
                )
                dst[c : c + CHUNK, :half] = jnp.where(keep, a, b)
                dst[c : c + CHUNK, half:] = jnp.where(keep, b, d)
        for m in range(MODES):
            for c in range(0, half, CHUNK):
                w = []
                for o in (c, c + half):
                    a, b = pr[m, o : o + CHUNK], pi[m, o : o + CHUNK]
                    u, v = pat_r[o : o + CHUNK], pat_i[o : o + CHUNK]
                    w.append((a * u - b * v, a * v + b * u))
                (tr, ti), (br, bi) = w
                xp[m, c : c + CHUNK] = (tr + br).astype(BF16)
                xp[m, c + half : c + half + CHUNK] = (ti + bi).astype(BF16)
                xq[m, c : c + CHUNK] = (tr - br).astype(BF16)
                xq[m, c + half : c + half + CHUNK] = (ti - bi).astype(BF16)
        for m in range(MODES):
            xe, xo = [], []
            for h in (dot(tab[0], xp[m]), dot(tab[2], xq[m])):
                hr, hi = h[:half], h[half:]
                xe.append(
                    jnp.concatenate(
                        [hr[:, :half] + hr[:, half:], hi[:, :half] + hi[:, half:]], axis=1
                    ).astype(BF16)
                )
                xo.append(
                    jnp.concatenate(
                        [hr[:, :half] - hr[:, half:], hi[:, :half] - hi[:, half:]], axis=1
                    ).astype(BF16)
                )
            fe = dot(jnp.concatenate(xe, axis=0), tab[1])
            fo = dot(jnp.concatenate(xo, axis=0), tab[3])
            far_e[m] = fe
            far_o[m] = fo
            te = fe[:, :half] * fe[:, :half] + fe[:, half:] * fe[:, half:]
            to = fo[:, :half] * fo[:, :half] + fo[:, half:] * fo[:, half:]
            if m == 0:
                inten[:, :half] = te
                inten[:, half:] = to
            else:
                inten[:, :half] += te
                inten[:, half:] += to
        for c in range(0, SIZE, CHUNK):
            rows = slice(c, c + CHUNK)
            inten[rows] = 1.0 - amp[s, rows] * lax.rsqrt(jnp.maximum(inten[rows], 0.25))
        for m in range(MODES):
            for p, dst in ((0, xp), (1, xq)):
                for c in range(0, half, CHUNK):
                    rows = slice(p * half + c, p * half + c + CHUNK)
                    f0, f1 = inten[rows, :half], inten[rows, half:]
                    e, o = far_e[m, rows], far_o[m, rows]
                    dst[m, c : c + CHUNK] = jnp.concatenate(
                        [e[:, :half] * f0, o[:, :half] * f1], axis=1
                    ).astype(BF16)
                    dst[m, c + half : c + half + CHUNK] = jnp.concatenate(
                        [e[:, half:] * f0, o[:, half:] * f1], axis=1
                    ).astype(BF16)
        for m in range(MODES):
            a = dot(tab[1], xp[m])
            b = dot(tab[3], xq[m])
            ur = jnp.concatenate([a[:half] + b[:half], a[:half] - b[:half]], axis=0).astype(BF16)
            ui = jnp.concatenate([a[half:] + b[half:], a[half:] - b[half:]], axis=0).astype(BF16)
            ga = dot(jnp.concatenate([ur[:, :half], ui[:, :half]], axis=1), tab[0])
            gb = dot(jnp.concatenate([ur[:, half:], ui[:, half:]], axis=1), tab[2])
            for c in range(0, SIZE, CHUNK):
                rows = slice(c, c + CHUNK)
                sm, df = ga[rows] + gb[rows], ga[rows] - gb[rows]
                gr = jnp.concatenate([sm[:, :half], df[:, :half]], axis=1)
                gi = jnp.concatenate([sm[:, half:], df[:, half:]], axis=1)
                a, b = pr[m, rows], pi[m, rows]
                u, v = pat_r[rows], pat_i[rows]
                obr = a * gr + b * gi
                obi = a * gi - b * gr
                if m == 0:
                    og_r[rows] = obr
                    og_i[rows] = obi
                else:
                    og_r[rows] += obr
                    og_i[rows] += obi
                pg[0, m, rows] += u * gr + v * gi
                pg[1, m, rows] += u * gi - v * gr
        low = lane < sh
        for part, src in ((0, og_r), (1, og_i)):
            for c in range(0, SIZE, CHUNK):
                a = pltpu.roll(src[c : c + CHUNK, :half], sh, 1)
                b = pltpu.roll(src[c : c + CHUNK, half:], sh, 1)
                acc[part, jb, pl.ds(y + c, CHUNK), :] += jnp.where(low, 0.0, a)
                acc[part, jb + 1, pl.ds(y + c, CHUNK), :] += jnp.where(low, a, b)
                acc[part, jb + 2, pl.ds(y + c, CHUNK), :] += jnp.where(low, b, 0.0)
        return carry

    lax.fori_loop(0, cnt[0], frame, 0)


def combine_kernel(
    rows,
    cols,
    step,
    acc,
    pg,
    obj_r,
    obj_i,
    pr,
    pi,
    new_r,
    new_i,
    new_pr,
    new_pi,
    tile,
    band,
    corner,
    side,
    below,
    data,
    result,
    rbuf0,
    rbuf1,
    rbuf2,
    rbuf3,
    local_sem,
    halo_send,
    halo_recv,
    sum_send,
    sum_recv,
):
    row, col = grid_place()
    n = 4
    core, x = lax.rem(col, 2), col // 2
    z, y = lax.rem(row, n), row // n
    up = (lax.rem(row + rows - 1, rows), col)
    down = (lax.rem(row + 1, rows), col)
    left = (row, lax.rem(col + cols - 1, cols))
    right = (row, lax.rem(col + 1, cols))
    other = (row, x * 2 + 1 - core)

    def peer(axis, k):
        if axis == "x":
            return (row, lax.rem(x + k, n) * 2 + core)
        if axis == "y":
            return (lax.rem(y + k, n) * n + z, col)
        return (y * n + lax.rem(z + k, n), col)

    where = {"x": x, "y": y, "z": z}
    peers = [peer(axis, k) for axis in "xyz" for k in (1, 2, 3)]

    loads = [
        pltpu.make_async_copy(pg, data, local_sem.at[0]),
        pltpu.make_async_copy(
            acc.at[:, pl.ds(0, 2), pl.ds(TILE, SIZE), :], band, local_sem.at[1]
        ),
        pltpu.make_async_copy(
            acc.at[:, pl.ds(0, 4), pl.ds(0, TILE), :], tile, local_sem.at[2]
        ),
    ]
    for copy in loads:
        copy.start()
    greet([up, down, left, right, other] + peers)

    def halo(src, dst, number, device):
        return pltpu.make_async_remote_copy(
            src_ref=src,
            dst_ref=dst,
            send_sem=halo_send.at[number],
            recv_sem=halo_recv.at[number],
            device_id=device,
            device_id_type=MESH,
        )

    corner_copy = halo(acc.at[:, pl.ds(4, 2), pl.ds(TILE, SIZE), :], corner, 0, right)
    far_copy = halo(
        acc.at[:, pl.ds(2, 2), pl.ds(TILE, SIZE), :], below.at[:, pl.ds(2, 2)], 1, down
    )
    near_copy = halo(band, below.at[:, pl.ds(0, 2)], 2, down)
    side_copy = halo(acc.at[:, pl.ds(4, 2), pl.ds(0, TILE), :], side, 3, right)
    corner_copy.start()
    far_copy.start()

    numbers = iter(range(64))

    def send(src, dst, device):
        number = next(numbers)
        copy = pltpu.make_async_remote_copy(
            src_ref=src,
            dst_ref=dst,
            send_sem=sum_send.at[number],
            recv_sem=sum_recv.at[number],
            device_id=device,
            device_id_type=MESH,
        )
        copy.start()
        return copy

    pending = []
    whole = 2 * MODES * SIZE
    kept = whole // 2
    mine = pl.multiple_of(core * kept, kept)
    theirs = pl.multiple_of((1 - core) * kept, kept)
    loads[0].wait()
    copy = send(data.at[pl.ds(theirs, kept), :], rbuf0, other)
    side_copy.start()
    copy.wait_recv()
    pending.append(copy)

    def add_up(base, length, buffers):
        size = min(length, 128)

        def body(i, carry):
            at = pl.multiple_of(base + i * size, 8)
            total = data[pl.ds(at, size), :]
            for ref, start in buffers:
                total += ref[pl.ds(pl.multiple_of(start + i * size, 8), size), :]
            data[pl.ds(at, size), :] = total
            return carry

        lax.fori_loop(0, length // size, body, 0)

    add_up(mine, kept, [(rbuf0, 0)])

    routes = ("yxz", "xyz")
    length = kept // len(routes)
    bases = [mine + part * length for part in range(len(routes))]
    trail = []
    for stage, buffer in enumerate((rbuf1, rbuf2, rbuf3)):
        quarter = length // n
        batch = []
        for part, route in enumerate(routes):
            axis = route[stage]
            p = where[axis]
            for k in (1, 2, 3):
                q = lax.rem(p + k, n)
                src = data.at[pl.ds(pl.multiple_of(bases[part] + q * quarter, 8), quarter), :]
                dst = buffer.at[pl.ds((part * 3 + k - 1) * quarter, quarter), :]
                batch.append(send(src, dst, peer(axis, k)))
        if stage == 0:
            loads[1].wait()
            corner_copy.wait_recv()
            for part in range(2):
                for j in range(2):
                    band[part, j] += corner[part, j]
            near_copy.start()
        trail.append(list(bases))
        for part, route in enumerate(routes):
            for k in range(3):
                batch[part * 3 + k].wait_recv()
            bases[part] = bases[part] + where[route[stage]] * quarter
            add_up(
                bases[part],
                quarter,
                [(buffer, (part * 3 + k) * quarter) for k in range(3)],
            )
        pending += batch
        length = quarter

    for part in range(len(routes)):
        at = pl.multiple_of(bases[part], 8)
        result[pl.ds(at, length), :] = data[pl.ds(at, length), :]
    for stage in (2, 1, 0):
        batch = []
        for part, route in enumerate(routes):
            axis = route[stage]
            for k in (1, 2, 3):
                here = result.at[pl.ds(pl.multiple_of(bases[part], 8), length), :]
                batch.append(send(here, here, peer(axis, k)))
        for copy in batch:
            copy.wait_recv()
        pending += batch
        bases = trail[stage]
        length *= n
    here = result.at[pl.ds(mine, kept), :]
    copy = send(here, here, other)
    pending.append(copy)

    far_copy.wait_recv()
    near_copy.wait_recv()
    side_copy.wait_recv()
    loads[2].wait()
    for part, obj, new in ((0, obj_r, new_r), (1, obj_i, new_i)):
        for j in range(4):
            lanes = slice(j * LANES, (j + 1) * LANES)
            for top in (0, SIZE):
                total = tile[part, j, top : top + SIZE]
                if top == 0:
                    total += below[part, j]
                if j < 2:
                    total += side[part, j, top : top + SIZE]
                new[top : top + SIZE, lanes] = obj[top : top + SIZE, lanes] - OBJECT_STEP * total

    copy.wait_recv()
    for part, old, new in ((0, pr, new_pr), (1, pi, new_pi)):
        for m in range(MODES):
            at = (part * MODES + m) * SIZE
            new[m] = old[m] - step * result[at : at + SIZE]
    for copy in pending:
        copy.wait_send()
    for copy in (corner_copy, far_copy, near_copy, side_copy):
        copy.wait_send()


def shards(object_real, object_imag, probe_real, probe_imag, amplitudes, positions, counts):
    rows, cols = lax.axis_size("row"), lax.axis_size("col")
    vmem = pl.BlockSpec(memory_space=pltpu.VMEM)
    smem = pl.BlockSpec(memory_space=pltpu.SMEM)
    anywhere = pl.BlockSpec(memory_space=pl.ANY)
    dma = pltpu.SemaphoreType.DMA
    extended = jax.ShapeDtypeStruct((2, 6, SPAN, LANES), F32)
    frame_shape = (SIZE, SIZE)

    ext, amp = pl.pallas_call(
        lambda *refs: halo_kernel(rows, cols, *refs),
        out_shape=(extended, jax.ShapeDtypeStruct((SLOTS, SIZE, SIZE), F32)),
        in_specs=[anywhere, anywhere, vmem, vmem],
        out_specs=(anywhere, vmem),
        scratch_shapes=[dma((8,)), dma((16,)), dma((16,))],
        compiler_params=pltpu.CompilerParams(
            collective_id=0, has_side_effects=True, vmem_limit_bytes=VMEM_LIMIT
        ),
        name="halo",
    )(object_real, object_imag, amplitudes[0, 0], jnp.asarray(parity_order()))

    acc, pg = pl.pallas_call(
        frames_kernel,
        out_shape=(extended, jax.ShapeDtypeStruct((2, MODES, SIZE, SIZE), F32)),
        in_specs=[smem, smem] + [vmem] * 5,
        out_specs=(vmem, vmem),
        scratch_shapes=[
            pltpu.VMEM(frame_shape, F32),
            pltpu.VMEM(frame_shape, F32),
            pltpu.VMEM((MODES, SIZE, SIZE), BF16),
            pltpu.VMEM((MODES, SIZE, SIZE), BF16),
            pltpu.VMEM((MODES, SIZE, SIZE), F32),
            pltpu.VMEM((MODES, SIZE, SIZE), F32),
            pltpu.VMEM(frame_shape, F32),
            pltpu.VMEM(frame_shape, F32),
            pltpu.VMEM(frame_shape, F32),
        ],
        compiler_params=pltpu.CompilerParams(vmem_limit_bytes=VMEM_LIMIT),
        name="frames",
    )(
        positions[0, 0].reshape(-1),
        counts.reshape(-1),
        ext,
        amp,
        probe_real,
        probe_imag,
        jnp.asarray(tables()),
    )

    step = PROBE_STEP / math.sqrt(SLOTS * rows * cols)
    tile_shape = jax.ShapeDtypeStruct((TILE, TILE), F32)
    probe_shape = jax.ShapeDtypeStruct((MODES, SIZE, SIZE), F32)
    whole = 2 * MODES * SIZE
    return pl.pallas_call(
        lambda *refs: combine_kernel(rows, cols, step, *refs),
        out_shape=(tile_shape, tile_shape, probe_shape, probe_shape),
        in_specs=[anywhere, anywhere] + [vmem] * 4,
        out_specs=(vmem,) * 4,
        scratch_shapes=[
            pltpu.VMEM((2, 4, TILE, LANES), F32),
            pltpu.VMEM((2, 2, SIZE, LANES), F32),
            pltpu.VMEM((2, 2, SIZE, LANES), F32),
            pltpu.VMEM((2, 2, TILE, LANES), F32),
            pltpu.VMEM((2, 4, SIZE, LANES), F32),
            pltpu.VMEM((whole, SIZE), F32),
            pltpu.VMEM((whole, SIZE), F32),
            pltpu.VMEM((whole // 2, SIZE), F32),
            pltpu.VMEM((whole // 2 * 3 // 4, SIZE), F32),
            pltpu.VMEM((whole // 8 * 3 // 4, SIZE), F32),
            pltpu.VMEM((whole // 32 * 3 // 4, SIZE), F32),
            dma((3,)),
            dma((4,)),
            dma((4,)),
            dma((38,)),
            dma((38,)),
        ],
        compiler_params=pltpu.CompilerParams(
            collective_id=1, has_side_effects=True, vmem_limit_bytes=VMEM_LIMIT
        ),
        name="combine",
    )(
        acc,
        pg.reshape(whole, SIZE),
        object_real,
        object_imag,
        probe_real,
        probe_imag,
    )


def solution(mesh):
    in_specs = (
        P("row", "col"),
        P("row", "col"),
        P(),
        P(),
        P("row", "col", None, None, None),
        P("row", "col", None, None),
        P("row", "col"),
    )
    out_specs = (P("row", "col"), P("row", "col"), P(), P())
    return jax.shard_map(shards, mesh=mesh, in_specs=in_specs, out_specs=out_specs, check_vma=False)
```

```python
import math

import jax
import jax.numpy as jnp
import numpy as np
from jax import lax
from jax.experimental import pallas as pl
from jax.experimental.pallas import tpu as pltpu
from jax.sharding import PartitionSpec as P

OBJECT_STEP = 0.25
PROBE_STEP = 0.5
MESH = pl.DeviceIdType.MESH
F32 = jnp.float32
BF16 = jnp.bfloat16
LANES = 128
SIZE = 256
MODES = 4
TILE = 512
SPAN = TILE + SIZE
SLOTS = 8
CHUNK = 32
VMEM_LIMIT = 56 * 2**20
SCHEDULE = (
    ("corner", ("far", 0)),
    (),
    (("side", 0),),
    (),
    (("far", 1), ("near", 0)),
    (("near", 1), ("side", 1)),
)


def tables():
    index = np.arange(SIZE)
    angle = (index[:, None] * index[None, :] % SIZE) * (2.0 * math.pi / SIZE)
    scale = 1.0 / math.sqrt(SIZE)
    cos_t = (np.cos(angle) * scale).astype(BF16)
    sin_t = (-np.sin(angle) * scale).astype(BF16)
    found = []
    for parity in range(2):
        c = cos_t[parity::2, : SIZE // 2]
        s = sin_t[parity::2, : SIZE // 2]
        table = np.block([[c, -s], [s, c]])
        found += [table, np.ascontiguousarray(table.T)]
    return np.stack(found)


def parity_order():
    order = np.concatenate([np.arange(0, SIZE, 2), np.arange(1, SIZE, 2)])
    right = np.arange(SIZE)[:, None] == order[None, :]
    return np.stack([right, right.T]).astype(BF16)


def dot(a, b):
    return jnp.dot(a, b, preferred_element_type=F32)


def grid_place():
    return lax.axis_index("row"), lax.axis_index("col")


def greet(peers):
    barrier = pltpu.get_barrier_semaphore()
    for peer in peers:
        pl.semaphore_signal(barrier, inc=1, device_id=peer, device_id_type=MESH)
    pl.semaphore_wait(barrier, len(peers))


def halo_kernel(rows, cols, obj_r, obj_i, amp, order, lower, wide, amp_out, send_sem, recv_sem):
    row, col = grid_place()
    up = (lax.rem(row + rows - 1, rows), col)
    down = (lax.rem(row + 1, rows), col)
    left = (row, lax.rem(col + cols - 1, cols))
    right = (row, lax.rem(col + 1, cols))
    greet((up, down, left, right))
    objs = (obj_r, obj_i)

    def band(part, j, number):
        return pltpu.make_async_remote_copy(
            src_ref=objs[part].at[pl.ds(0, SIZE), pl.ds(j * LANES, LANES)],
            dst_ref=lower.at[part, j],
            send_sem=send_sem.at[number],
            recv_sem=recv_sem.at[number],
            device_id=up,
            device_id_type=MESH,
        )

    def side(part, j, number):
        return pltpu.make_async_remote_copy(
            src_ref=objs[part].at[:, pl.ds(j * LANES, LANES)],
            dst_ref=wide.at[part, j, pl.ds(0, TILE), :],
            send_sem=send_sem.at[number],
            recv_sem=recv_sem.at[number],
            device_id=left,
            device_id_type=MESH,
        )

    def corner(part, j, number):
        return pltpu.make_async_remote_copy(
            src_ref=lower.at[part, j],
            dst_ref=wide.at[part, j, pl.ds(TILE, SIZE), :],
            send_sem=send_sem.at[number],
            recv_sem=recv_sem.at[number],
            device_id=left,
            device_id_type=MESH,
        )

    bands = [band(part, j, 2 * j + part) for j in range(4) for part in range(2)]
    sides = [side(part, j, 8 + 2 * j + part) for j in range(2) for part in range(2)]
    corners = [corner(part, j, 12 + 2 * j + part) for j in range(2) for part in range(2)]
    for copy in bands + sides:
        copy.start()

    def sort(slot, carry):
        a = amp[slot]
        by_row = jnp.zeros((SIZE, SIZE), F32)
        for step in range(3):
            piece = a.astype(BF16)
            by_row += dot(order[1], piece)
            a = a - piece.astype(F32)
        total = jnp.zeros((SIZE, SIZE), F32)
        for step in range(3):
            piece = by_row.astype(BF16)
            total += dot(piece, order[0])
            by_row = by_row - piece.astype(F32)
        amp_out[slot] = total
        return carry

    lax.fori_loop(0, SLOTS, sort, 0)
    for number in range(4):
        bands[number].wait_recv()
        corners[number].start()
    for copy in bands:
        copy.wait_send()
    for copy in bands[4:]:
        copy.wait_recv()
    for copy in sides + corners:
        copy.wait()


def frames_kernel(
    pos,
    cnt,
    obj_r,
    obj_i,
    lower,
    wide,
    amp,
    pr,
    pi,
    tab,
    acc,
    pg,
    ext,
    pat_r,
    pat_i,
    xp,
    xq,
    xe,
    xo,
    far_e,
    far_o,
    inten,
    og_r,
    og_i,
    sem,
):
    half = SIZE // 2
    loads = [
        pltpu.make_async_copy(lower, ext.at[:, pl.ds(0, 4), pl.ds(TILE, SIZE), :], sem.at[0]),
        pltpu.make_async_copy(wide, ext.at[:, pl.ds(4, 2)], sem.at[1]),
    ]
    for part, obj in ((0, obj_r), (1, obj_i)):
        for j in range(4):
            loads.append(
                pltpu.make_async_copy(
                    obj.at[:, pl.ds(j * LANES, LANES)],
                    ext.at[part, j, pl.ds(0, TILE), :],
                    sem.at[2 + 4 * part + j],
                )
            )
    for copy in loads:
        copy.start()
    blank = jnp.zeros((SPAN, LANES), F32)
    for part in range(2):
        for j in range(6):
            acc[part, j] = blank
        for m in range(MODES):
            pg[part, m] = jnp.zeros((SIZE, SIZE), F32)
    for copy in loads:
        copy.wait()

    def frame(s, carry):
        y = pos[2 * s]
        x = pos[2 * s + 1]
        jb = x // LANES
        sh = x % LANES
        back = (LANES - sh) % LANES
        lane = lax.broadcasted_iota(jnp.int32, (CHUNK, LANES), 1)
        keep = lane < LANES - sh
        for part, dst in ((0, pat_r), (1, pat_i)):
            for c in range(0, SIZE, CHUNK):
                a, b, d = (
                    pltpu.roll(ext[part, jb + t, pl.ds(y + c, CHUNK), :], back, 1) for t in range(3)
                )
                dst[c : c + CHUNK, :half] = jnp.where(keep, a, b)
                dst[c : c + CHUNK, half:] = jnp.where(keep, b, d)
        for m in range(MODES):
            for c in range(0, half, CHUNK):
                w = []
                for o in (c, c + half):
                    a, b = pr[m, o : o + CHUNK], pi[m, o : o + CHUNK]
                    u, v = pat_r[o : o + CHUNK], pat_i[o : o + CHUNK]
                    w.append((a * u - b * v, a * v + b * u))
                (tr, ti), (br, bi) = w
                xp[m, c : c + CHUNK] = (tr + br).astype(BF16)
                xp[m, c + half : c + half + CHUNK] = (ti + bi).astype(BF16)
                xq[m, c : c + CHUNK] = (tr - br).astype(BF16)
                xq[m, c + half : c + half + CHUNK] = (ti - bi).astype(BF16)
        for m in range(MODES):
            for p, src in ((0, xp), (1, xq)):
                h = dot(tab[2 * p], src[m])
                rows = slice(m * SIZE + p * half, m * SIZE + (p + 1) * half)
                for part in range(2):
                    first, second = h[part * half : (part + 1) * half, :half], h[part * half : (part + 1) * half, half:]
                    lanes = slice(part * half, (part + 1) * half)
                    xe[rows, lanes] = (first + second).astype(BF16)
                    xo[rows, lanes] = (first - second).astype(BF16)
        far_e[...] = dot(xe[...], tab[1]).reshape(MODES, SIZE, SIZE)
        far_o[...] = dot(xo[...], tab[3]).reshape(MODES, SIZE, SIZE)
        for c in range(0, SIZE, CHUNK):
            rows = slice(c, c + CHUNK)
            for far, lanes in ((far_e, slice(0, half)), (far_o, slice(half, SIZE))):
                total = None
                for m in range(MODES):
                    f = far[m, rows]
                    f = f * f
                    f = f[:, :half] + f[:, half:]
                    total = f if total is None else total + f
                inten[rows, lanes] = 1.0 - amp[s, rows, lanes] * lax.rsqrt(jnp.maximum(total, 0.25))
        for m in range(MODES):
            for p, dst in ((0, xp), (1, xq)):
                for c in range(0, half, CHUNK):
                    rows = slice(p * half + c, p * half + c + CHUNK)
                    f0, f1 = inten[rows, :half], inten[rows, half:]
                    e, o = far_e[m, rows], far_o[m, rows]
                    dst[m, c : c + CHUNK] = jnp.concatenate(
                        [e[:, :half] * f0, o[:, :half] * f1], axis=1
                    ).astype(BF16)
                    dst[m, c + half : c + half + CHUNK] = jnp.concatenate(
                        [e[:, half:] * f0, o[:, half:] * f1], axis=1
                    ).astype(BF16)
        for m in range(MODES):
            a = dot(tab[1], xp[m])
            b = dot(tab[3], xq[m])
            for p, v in ((0, a + b), (1, a - b)):
                v = v.astype(BF16)
                rows = slice(m * SIZE + p * half, m * SIZE + (p + 1) * half)
                xe[rows, :half] = v[:half, :half]
                xe[rows, half:] = v[half:, :half]
                xo[rows, :half] = v[:half, half:]
                xo[rows, half:] = v[half:, half:]
        far_e[...] = dot(xe[...], tab[0]).reshape(MODES, SIZE, SIZE)
        far_o[...] = dot(xo[...], tab[2]).reshape(MODES, SIZE, SIZE)
        for c in range(0, SIZE, CHUNK):
            rows = slice(c, c + CHUNK)
            u, v = pat_r[rows], pat_i[rows]
            sum_r = sum_i = None
            for m in range(MODES):
                ga, gb = far_e[m, rows], far_o[m, rows]
                sm, df = ga + gb, ga - gb
                gr = jnp.concatenate([sm[:, :half], df[:, :half]], axis=1)
                gi = jnp.concatenate([sm[:, half:], df[:, half:]], axis=1)
                a, b = pr[m, rows], pi[m, rows]
                obr = a * gr + b * gi
                obi = a * gi - b * gr
                sum_r = obr if sum_r is None else sum_r + obr
                sum_i = obi if sum_i is None else sum_i + obi
                pg[0, m, rows] += u * gr + v * gi
                pg[1, m, rows] += u * gi - v * gr
            og_r[rows] = sum_r
            og_i[rows] = sum_i
        low = lane < sh
        for part, src in ((0, og_r), (1, og_i)):
            for c in range(0, SIZE, CHUNK):
                a = pltpu.roll(src[c : c + CHUNK, :half], sh, 1)
                b = pltpu.roll(src[c : c + CHUNK, half:], sh, 1)
                acc[part, jb, pl.ds(y + c, CHUNK), :] += jnp.where(low, 0.0, a)
                acc[part, jb + 1, pl.ds(y + c, CHUNK), :] += jnp.where(low, a, b)
                acc[part, jb + 2, pl.ds(y + c, CHUNK), :] += jnp.where(low, b, 0.0)
        return carry

    lax.fori_loop(0, cnt[0], frame, 0)


def combine_kernel(
    rows,
    cols,
    acc,
    pg,
    below,
    side,
    result,
    band,
    corner,
    data,
    rbuf0,
    rbuf1,
    rbuf2,
    local_sem,
    halo_send,
    halo_recv,
    sum_send,
    sum_recv,
):
    row, col = grid_place()
    n = 4
    core, x = lax.rem(col, 2), col // 2
    z, y = lax.rem(row, n), row // n
    up = (lax.rem(row + rows - 1, rows), col)
    down = (lax.rem(row + 1, rows), col)
    left = (row, lax.rem(col + cols - 1, cols))
    right = (row, lax.rem(col + 1, cols))
    other = (row, x * 2 + 1 - core)

    def at_place(dx, dy, dz):
        return (
            lax.rem(y + dy, n) * n + lax.rem(z + dz, n),
            lax.rem(x + dx, n) * 2 + core,
        )

    steps = [(a, b) for a in range(n) for b in range(n) if a or b]
    lines = ([at_place(0, k, 0) for k in (1, 2, 3)], [at_place(k, 0, 0) for k in (1, 2, 3)])
    planes = ([at_place(a, 0, b) for a, b in steps], [at_place(0, a, b) for a, b in steps])
    line_at = (y, x)
    plane_at = (x, y)

    loads = [
        pltpu.make_async_copy(pg, data, local_sem.at[0]),
        pltpu.make_async_copy(
            acc.at[:, pl.ds(0, 2), pl.ds(TILE, SIZE), :], band, local_sem.at[1]
        ),
    ]
    for copy in loads:
        copy.start()
    greet(
        [up, down, left, right, other]
        + planes[0]
        + [p for p, (a, b) in zip(planes[1], steps) if a]
    )

    def halo(src, dst, number, device):
        return pltpu.make_async_remote_copy(
            src_ref=src,
            dst_ref=dst,
            send_sem=halo_send.at[number],
            recv_sem=halo_recv.at[number],
            device_id=device,
            device_id_type=MESH,
        )

    corner_copy = halo(acc.at[:, pl.ds(4, 2), pl.ds(TILE, SIZE), :], corner, 0, right)
    moves = {"corner": corner_copy}
    for part in range(2):
        moves["far", part] = halo(
            acc.at[part, pl.ds(2, 2), pl.ds(TILE, SIZE), :], below.at[part, pl.ds(2, 2)], 1 + part, down
        )
        moves["near", part] = halo(band.at[part], below.at[part, pl.ds(0, 2)], 3 + part, down)
        moves["side", part] = halo(
            acc.at[part, pl.ds(4, 2), pl.ds(0, TILE), :], side.at[part], 5 + part, right
        )

    def begin(stage):
        for name in SCHEDULE[stage]:
            moves[name].start()

    begin(0)

    numbers = iter(range(82))
    pending = []

    def send(src, dst, device):
        number = next(numbers)
        copy = pltpu.make_async_remote_copy(
            src_ref=src,
            dst_ref=dst,
            send_sem=sum_send.at[number],
            recv_sem=sum_recv.at[number],
            device_id=device,
            device_id_type=MESH,
        )
        copy.start()
        pending.append(copy)
        return copy

    def aligned(start, size):
        return pl.ds(pl.multiple_of(start, 8), size)

    whole = 2 * MODES * SIZE
    kept = whole // 2
    part_rows = kept // 2
    quarter = part_rows // n
    piece = quarter // (n * n)
    mine = core * kept
    theirs = (1 - core) * kept
    loads[0].wait()
    core_copies = [
        send(
            data.at[aligned(theirs + part * part_rows, part_rows), :],
            rbuf0.at[pl.ds(part * part_rows, part_rows), :],
            other,
        )
        for part in range(2)
    ]

    begin(1)
    line_copies = []
    for part in range(2):
        core_copies[part].wait_recv()
        base = mine + part * part_rows

        def add_core(i, carry, base=base, part=part):
            here = aligned(base + i * quarter, quarter)
            data[here, :] += rbuf0[pl.ds(pl.multiple_of(part * part_rows + i * quarter, 8), quarter), :]
            return carry

        lax.fori_loop(0, n, add_core, 0)
        for k in (1, 2, 3):
            q = lax.rem(line_at[part] + k, n)
            line_copies.append(
                send(
                    data.at[aligned(base + q * quarter, quarter), :],
                    rbuf1.at[pl.ds((part * 3 + k - 1) * quarter, quarter), :],
                    lines[part][k - 1],
                )
            )

    loads[1].wait()
    corner_copy.wait_recv()
    for part in range(2):
        for j in range(2):
            band[part, j] += corner[part, j]
    begin(2)

    bases = []
    plane_copies = []
    for part in range(2):
        for k in range(3):
            line_copies[part * 3 + k].wait_recv()
        base = mine + part * part_rows + line_at[part] * quarter
        bases.append(base)
        here = aligned(base, quarter)
        total = data[here, :]
        for k in range(3):
            total += rbuf1[(part * 3 + k) * quarter : (part * 3 + k + 1) * quarter, :]
        data[here, :] = total
        for k, (a, b) in enumerate(steps):
            q = lax.rem(plane_at[part] + a, n) * n + lax.rem(z + b, n)
            plane_copies.append(
                send(
                    data.at[aligned(base + q * piece, piece), :],
                    rbuf2.at[pl.ds((part * 15 + k) * piece, piece), :],
                    planes[part][k],
                )
            )
    begin(3)

    gather_copies = []
    for part in range(2):
        for k in range(15):
            plane_copies[part * 15 + k].wait_recv()
        here = aligned(bases[part] + (plane_at[part] * n + z) * piece, piece)
        total = data[here, :]
        for k in range(15):
            total += rbuf2[(part * 15 + k) * piece : (part * 15 + k + 1) * piece, :]
        result[here, :] = total
        for k in range(15):
            gather_copies.append(
                send(result.at[here, :], result.at[here, :], planes[part][k])
            )

    begin(4)
    line_copies = []
    for part in range(2):
        for k in range(15):
            gather_copies[part * 15 + k].wait_recv()
        here = result.at[aligned(bases[part], quarter), :]
        for k in (1, 2, 3):
            line_copies.append(send(here, here, lines[part][k - 1]))
    core_copies = []
    for part in range(2):
        here = result.at[aligned(bases[part], quarter), :]
        core_copies.append(send(here, here, other))
    begin(5)
    for k in (1, 3, 2):
        for part in range(2):
            line_copies[part * 3 + k - 1].wait_recv()
            q = lax.rem(line_at[part] + n - k, n)
            here = result.at[aligned(mine + part * part_rows + q * quarter, quarter), :]
            core_copies.append(send(here, here, other))
    for copy in core_copies:
        copy.wait_recv()
    for copy in pending:
        copy.wait_send()
    for name, copy in moves.items():
        if name != "corner":
            copy.wait_recv()
    for copy in moves.values():
        copy.wait_send()


def finish_kernel(step, acc, below, side, result, obj_r, obj_i, pr, pi, new_r, new_i, new_pr, new_pi):
    upper = pl.program_id(0) < 2
    for part, obj, new in ((0, obj_r, new_r), (1, obj_i, new_i)):
        for j in range(4):
            lanes = slice(j * LANES, (j + 1) * LANES)
            total = acc[part, j] + jnp.where(upper, below[part, j], 0.0)
            if j < 2:
                total += side[part, j]
            new[:, lanes] = obj[:, lanes] - OBJECT_STEP * total
    for part, old, new in ((0, pr, new_pr), (1, pi, new_pi)):
        new[0] = old[0] - step * result[part, 0]


def shards(object_real, object_imag, probe_real, probe_imag, amplitudes, positions, counts):
    rows, cols = lax.axis_size("row"), lax.axis_size("col")
    vmem = pl.BlockSpec(memory_space=pltpu.VMEM)
    smem = pl.BlockSpec(memory_space=pltpu.SMEM)
    anywhere = pl.BlockSpec(memory_space=pl.ANY)
    dma = pltpu.SemaphoreType.DMA
    extended = jax.ShapeDtypeStruct((2, 6, SPAN, LANES), F32)
    frame_shape = (SIZE, SIZE)

    lower, wide, amp = pl.pallas_call(
        lambda *refs: halo_kernel(rows, cols, *refs),
        out_shape=(
            jax.ShapeDtypeStruct((2, 4, SIZE, LANES), F32),
            jax.ShapeDtypeStruct((2, 2, SPAN, LANES), F32),
            jax.ShapeDtypeStruct((SLOTS, SIZE, SIZE), F32),
        ),
        in_specs=[anywhere, anywhere, vmem, vmem],
        out_specs=(anywhere, anywhere, vmem),
        scratch_shapes=[dma((16,)), dma((16,))],
        compiler_params=pltpu.CompilerParams(
            collective_id=0, has_side_effects=True, vmem_limit_bytes=16 * 2**20
        ),
        name="halo",
    )(object_real, object_imag, amplitudes[0, 0], jnp.asarray(parity_order()))

    acc, pg = pl.pallas_call(
        frames_kernel,
        out_shape=(extended, jax.ShapeDtypeStruct((2, MODES, SIZE, SIZE), F32)),
        in_specs=[smem, smem] + [anywhere] * 4 + [vmem] * 4,
        out_specs=(vmem, vmem),
        scratch_shapes=[
            pltpu.VMEM((2, 6, SPAN, LANES), F32),
            pltpu.VMEM(frame_shape, F32),
            pltpu.VMEM(frame_shape, F32),
            pltpu.VMEM((MODES, SIZE, SIZE), BF16),
            pltpu.VMEM((MODES, SIZE, SIZE), BF16),
            pltpu.VMEM((MODES * SIZE, SIZE), BF16),
            pltpu.VMEM((MODES * SIZE, SIZE), BF16),
            pltpu.VMEM((MODES, SIZE, SIZE), F32),
            pltpu.VMEM((MODES, SIZE, SIZE), F32),
            pltpu.VMEM(frame_shape, F32),
            pltpu.VMEM(frame_shape, F32),
            pltpu.VMEM(frame_shape, F32),
            dma((10,)),
        ],
        compiler_params=pltpu.CompilerParams(vmem_limit_bytes=32 * 2**20),
        name="frames",
    )(
        positions[0, 0].reshape(-1),
        counts.reshape(-1),
        object_real,
        object_imag,
        lower,
        wide,
        amp,
        probe_real,
        probe_imag,
        jnp.asarray(tables()),
    )

    step = PROBE_STEP / math.sqrt(SLOTS * rows * cols)
    tile_shape = jax.ShapeDtypeStruct((TILE, TILE), F32)
    probe_shape = jax.ShapeDtypeStruct((MODES, SIZE, SIZE), F32)
    whole = 2 * MODES * SIZE
    below, side, result = pl.pallas_call(
        lambda *refs: combine_kernel(rows, cols, *refs),
        out_shape=(
            jax.ShapeDtypeStruct((2, 4, SIZE, LANES), F32),
            jax.ShapeDtypeStruct((2, 2, TILE, LANES), F32),
            jax.ShapeDtypeStruct((whole, SIZE), F32),
        ),
        in_specs=[anywhere, anywhere],
        out_specs=(anywhere, anywhere, vmem),
        scratch_shapes=[
            pltpu.VMEM((2, 2, SIZE, LANES), F32),
            pltpu.VMEM((2, 2, SIZE, LANES), F32),
            pltpu.VMEM((whole, SIZE), F32),
            pltpu.VMEM((whole // 2, SIZE), F32),
            pltpu.VMEM((whole // 2 * 3 // 4, SIZE), F32),
            pltpu.VMEM((30 * whole // 256, SIZE), F32),
            dma((2,)),
            dma((7,)),
            dma((7,)),
            dma((82,)),
            dma((82,)),
        ],
        compiler_params=pltpu.CompilerParams(
            collective_id=1, has_side_effects=True, vmem_limit_bytes=16 * 2**20
        ),
        name="combine",
    )(acc, pg.reshape(whole, SIZE))

    part = TILE // 4
    tile_block = pl.BlockSpec((part, TILE), lambda i: (i, 0))
    probe_block = pl.BlockSpec((1, SIZE, SIZE), lambda i: (i, 0, 0))
    return pl.pallas_call(
        lambda *refs: finish_kernel(step, *refs),
        grid=(4,),
        out_shape=(tile_shape, tile_shape, probe_shape, probe_shape),
        in_specs=[
            pl.BlockSpec((2, 4, part, LANES), lambda i: (0, 0, i, 0)),
            pl.BlockSpec((2, 4, part, LANES), lambda i: (0, 0, jnp.minimum(i, 1), 0)),
            pl.BlockSpec((2, 2, part, LANES), lambda i: (0, 0, i, 0)),
            pl.BlockSpec((2, 1, SIZE, SIZE), lambda i: (0, i, 0, 0)),
            tile_block,
            tile_block,
            probe_block,
            probe_block,
        ],
        out_specs=(tile_block, tile_block, probe_block, probe_block),
        compiler_params=pltpu.CompilerParams(vmem_limit_bytes=16 * 2**20),
        name="finish",
    )(
        acc,
        below,
        side,
        result.reshape(2, MODES, SIZE, SIZE),
        object_real,
        object_imag,
        probe_real,
        probe_imag,
    )


def solution(mesh):
    in_specs = (
        P("row", "col"),
        P("row", "col"),
        P(),
        P(),
        P("row", "col", None, None, None),
        P("row", "col", None, None),
        P("row", "col"),
    )
    out_specs = (P("row", "col"), P("row", "col"), P(), P())
    return jax.shard_map(shards, mesh=mesh, in_specs=in_specs, out_specs=out_specs, check_vma=False)
```

```python
import math

import jax
import jax.numpy as jnp
import numpy as np
from jax import lax
from jax.experimental import pallas as pl
from jax.experimental.pallas import tpu as pltpu
from jax.sharding import PartitionSpec as P

OBJECT_STEP = 0.25
PROBE_STEP = 0.5
MESH = pl.DeviceIdType.MESH
F32 = jnp.float32
BF16 = jnp.bfloat16
LANES = 128
SIZE = 256
MODES = 4
TILE = 512
SPAN = TILE + SIZE
SLOTS = 8
CHUNK = 32
HALO_LIMIT = 56 * 2**20
LOWER = 0
WIDE = 8
AMPS = 20
BLOCKS = 288
SCHEDULE = (
    ("corner", ("far", 0)),
    (),
    (("far", 1),),
    (),
    (("near", 0), ("side", 0)),
    (("near", 1), ("side", 1)),
)


def tables():
    index = np.arange(SIZE)
    angle = (index[:, None] * index[None, :] % SIZE) * (2.0 * math.pi / SIZE)
    scale = 1.0 / math.sqrt(SIZE)
    cos_t = (np.cos(angle) * scale).astype(BF16)
    sin_t = (-np.sin(angle) * scale).astype(BF16)
    found = []
    for parity in range(2):
        c = cos_t[parity::2, : SIZE // 2]
        s = sin_t[parity::2, : SIZE // 2]
        table = np.block([[c, -s], [s, c]])
        found += [table, np.ascontiguousarray(table.T)]
    return np.stack(found)


def dot(a, b):
    return jnp.dot(a, b, preferred_element_type=F32)


def grid_place():
    return lax.axis_index("row"), lax.axis_index("col")


def greet(peers):
    barrier = pltpu.get_barrier_semaphore()
    for peer in peers:
        pl.semaphore_signal(barrier, inc=1, device_id=peer, device_id_type=MESH)
    pl.semaphore_wait(barrier, len(peers))


def halo_kernel(
    rows, cols, obj_r, obj_i, amp_in, mail, amp, sorted_amp, order, load_sem, store_sem, send_sem, recv_sem
):
    row, col = grid_place()
    up = (lax.rem(row + rows - 1, rows), col)
    down = (lax.rem(row + 1, rows), col)
    left = (row, lax.rem(col + cols - 1, cols))
    right = (row, lax.rem(col + 1, cols))
    loads = [pltpu.make_async_copy(amp_in.at[s], amp.at[s], load_sem.at[s]) for s in range(SLOTS)]
    for copy in loads:
        copy.start()
    greet((up, down, left, right))
    objs = (obj_r, obj_i)
    has_up, has_down, has_left, has_right = row > 0, row < rows - 1, col > 0, col < cols - 1

    def band(part, j, number):
        return pltpu.make_async_remote_copy(
            src_ref=objs[part].at[pl.ds(0, SIZE), pl.ds(j * LANES, LANES)],
            dst_ref=mail.at[LOWER + part * 4 + j],
            send_sem=send_sem.at[number],
            recv_sem=recv_sem.at[number],
            device_id=up,
            device_id_type=MESH,
        )

    def side(part, j, third, number):
        return pltpu.make_async_remote_copy(
            src_ref=objs[part].at[pl.ds(third * SIZE, SIZE), pl.ds(j * LANES, LANES)],
            dst_ref=mail.at[WIDE + (part * 2 + j) * 3 + third],
            send_sem=send_sem.at[number],
            recv_sem=recv_sem.at[number],
            device_id=left,
            device_id_type=MESH,
        )

    def corner(part, j, number):
        return pltpu.make_async_remote_copy(
            src_ref=mail.at[LOWER + part * 4 + j],
            dst_ref=mail.at[WIDE + (part * 2 + j) * 3 + 2],
            send_sem=send_sem.at[number],
            recv_sem=recv_sem.at[number],
            device_id=left,
            device_id_type=MESH,
        )

    bands = [band(part, j, 2 * j + part) for j in range(4) for part in range(2)]
    sides = [
        side(part, j, third, 8 + 4 * third + 2 * j + part)
        for third in range(2)
        for j in range(2)
        for part in range(2)
    ]
    corners = [corner(part, j, 16 + 2 * j + part) for j in range(2) for part in range(2)]

    @pl.when(has_up)
    def _():
        for copy in bands:
            copy.start()

    @pl.when(has_left)
    def _():
        for copy in sides:
            copy.start()

    half = SIZE // 2
    first = lax.broadcasted_iota(jnp.int32, (SIZE, SIZE), 0)
    second = lax.broadcasted_iota(jnp.int32, (SIZE, SIZE), 1)

    def source(i):
        return jnp.where(i < half, 2 * i, 2 * (i - half) + 1)

    order[0] = jnp.where(first == source(second), 1.0, 0.0).astype(BF16)
    order[1] = jnp.where(second == source(first), 1.0, 0.0).astype(BF16)
    for copy in loads:
        copy.wait()

    def sort(slot, carry):
        a = amp[slot]
        by_row = jnp.zeros((SIZE, SIZE), F32)
        for step in range(3):
            piece = a.astype(BF16)
            by_row += dot(order[1], piece)
            a = a - piece.astype(F32)
        total = jnp.zeros((SIZE, SIZE), F32)
        for step in range(3):
            piece = by_row.astype(BF16)
            total += dot(piece, order[0])
            by_row = by_row - piece.astype(F32)
        sorted_amp[2 * slot] = total[:, :half]
        sorted_amp[2 * slot + 1] = total[:, half:]
        return carry

    lax.fori_loop(0, SLOTS, sort, 0)
    store = pltpu.make_async_copy(sorted_amp, mail.at[pl.ds(AMPS, 2 * SLOTS)], store_sem)
    store.start()

    for number in range(4):

        @pl.when(has_down)
        def _():
            bands[number].wait_recv()

        @pl.when(has_down & has_left)
        def _():
            corners[number].start()

    @pl.when(has_down)
    def _():
        for copy in bands[4:]:
            copy.wait_recv()

    @pl.when(has_up)
    def _():
        for copy in bands:
            copy.wait_send()

    @pl.when(has_right)
    def _():
        for copy in sides:
            copy.wait_recv()

    @pl.when(has_left)
    def _():
        for copy in sides:
            copy.wait_send()

    @pl.when(has_down & has_right)
    def _():
        for copy in corners:
            copy.wait_recv()

    @pl.when(has_down & has_left)
    def _():
        for copy in corners:
            copy.wait_send()

    store.wait()


def frames_kernel(
    pos,
    cnt,
    obj_r,
    obj_i,
    mail,
    pr,
    pi,
    tab_in,
    acc,
    pg,
    tab,
    amp,
    ext,
    pat_r,
    pat_i,
    xp,
    xq,
    xe,
    xo,
    far_e,
    far_o,
    inten,
    og_r,
    og_i,
    sem,
):
    half = SIZE // 2
    loads = [
        pltpu.make_async_copy(
            mail.at[pl.ds(LOWER + 4 * part, 4)],
            ext.at[part, pl.ds(0, 4), pl.ds(TILE, SIZE), :],
            sem.at[part],
        )
        for part in range(2)
    ] + [
        pltpu.make_async_copy(
            mail.at[WIDE + (part * 2 + j) * 3 + third],
            ext.at[part, 4 + j, pl.ds(third * SIZE, SIZE), :],
            sem.at[12 + (part * 2 + j) * 3 + third],
        )
        for part in range(2)
        for j in range(2)
        for third in range(3)
    ]
    loads.append(pltpu.make_async_copy(mail.at[pl.ds(AMPS, 2 * SLOTS)], amp, sem.at[11]))
    loads.append(pltpu.make_async_copy(tab_in, tab, sem.at[10]))
    for part, obj in ((0, obj_r), (1, obj_i)):
        for j in range(4):
            loads.append(
                pltpu.make_async_copy(
                    obj.at[:, pl.ds(j * LANES, LANES)],
                    ext.at[part, j, pl.ds(0, TILE), :],
                    sem.at[2 + 4 * part + j],
                )
            )
    for copy in loads:
        copy.start()
    blank = jnp.zeros((SPAN, LANES), F32)
    for part in range(2):
        for j in range(6):
            acc[part, j] = blank
        for m in range(MODES):
            pg[part, m] = jnp.zeros((SIZE, SIZE), F32)
    for copy in loads:
        copy.wait()

    def frame(s, carry):
        y = pos[0, 0, s, 0]
        x = pos[0, 0, s, 1]
        jb = x // LANES
        sh = x % LANES
        back = (LANES - sh) % LANES
        lane = lax.broadcasted_iota(jnp.int32, (CHUNK, LANES), 1)
        keep = lane < LANES - sh
        for part, dst in ((0, pat_r), (1, pat_i)):
            for c in range(0, SIZE, CHUNK):
                a, b, d = (
                    pltpu.roll(ext[part, jb + t, pl.ds(y + c, CHUNK), :], back, 1) for t in range(3)
                )
                dst[c : c + CHUNK, :half] = jnp.where(keep, a, b)
                dst[c : c + CHUNK, half:] = jnp.where(keep, b, d)
        for m in range(MODES):
            for c in range(0, half, CHUNK):
                w = []
                for o in (c, c + half):
                    a, b = pr[m, o : o + CHUNK], pi[m, o : o + CHUNK]
                    u, v = pat_r[o : o + CHUNK], pat_i[o : o + CHUNK]
                    w.append((a * u - b * v, a * v + b * u))
                (tr, ti), (br, bi) = w
                xp[m, c : c + CHUNK] = (tr + br).astype(BF16)
                xp[m, c + half : c + half + CHUNK] = (ti + bi).astype(BF16)
                xq[m, c : c + CHUNK] = (tr - br).astype(BF16)
                xq[m, c + half : c + half + CHUNK] = (ti - bi).astype(BF16)
        for m in range(MODES):
            for p, src in ((0, xp), (1, xq)):
                h = dot(tab[2 * p], src[m])
                rows = slice(m * SIZE + p * half, m * SIZE + (p + 1) * half)
                for part in range(2):
                    first, second = h[part * half : (part + 1) * half, :half], h[part * half : (part + 1) * half, half:]
                    lanes = slice(part * half, (part + 1) * half)
                    xe[rows, lanes] = (first + second).astype(BF16)
                    xo[rows, lanes] = (first - second).astype(BF16)
        far_e[...] = dot(xe[...], tab[1]).reshape(MODES, SIZE, SIZE)
        far_o[...] = dot(xo[...], tab[3]).reshape(MODES, SIZE, SIZE)
        for c in range(0, SIZE, CHUNK):
            rows = slice(c, c + CHUNK)
            for side, far in enumerate((far_e, far_o)):
                total = None
                for m in range(MODES):
                    f = far[m, rows]
                    f = f * f
                    f = f[:, :half] + f[:, half:]
                    total = f if total is None else total + f
                inten[rows, side * half : (side + 1) * half] = 1.0 - amp[2 * s + side, rows] * lax.rsqrt(
                    jnp.maximum(total, 0.25)
                )
        for m in range(MODES):
            for p, dst in ((0, xp), (1, xq)):
                for c in range(0, half, CHUNK):
                    rows = slice(p * half + c, p * half + c + CHUNK)
                    f0, f1 = inten[rows, :half], inten[rows, half:]
                    e, o = far_e[m, rows], far_o[m, rows]
                    dst[m, c : c + CHUNK] = jnp.concatenate(
                        [e[:, :half] * f0, o[:, :half] * f1], axis=1
                    ).astype(BF16)
                    dst[m, c + half : c + half + CHUNK] = jnp.concatenate(
                        [e[:, half:] * f0, o[:, half:] * f1], axis=1
                    ).astype(BF16)
        for m in range(MODES):
            a = dot(tab[1], xp[m])
            b = dot(tab[3], xq[m])
            for p, v in ((0, a + b), (1, a - b)):
                v = v.astype(BF16)
                rows = slice(m * SIZE + p * half, m * SIZE + (p + 1) * half)
                xe[rows, :half] = v[:half, :half]
                xe[rows, half:] = v[half:, :half]
                xo[rows, :half] = v[:half, half:]
                xo[rows, half:] = v[half:, half:]
        far_e[...] = dot(xe[...], tab[0]).reshape(MODES, SIZE, SIZE)
        far_o[...] = dot(xo[...], tab[2]).reshape(MODES, SIZE, SIZE)
        for c in range(0, SIZE, CHUNK):
            rows = slice(c, c + CHUNK)
            u, v = pat_r[rows], pat_i[rows]
            sum_r = sum_i = None
            for m in range(MODES):
                ga, gb = far_e[m, rows], far_o[m, rows]
                sm, df = ga + gb, ga - gb
                gr = jnp.concatenate([sm[:, :half], df[:, :half]], axis=1)
                gi = jnp.concatenate([sm[:, half:], df[:, half:]], axis=1)
                a, b = pr[m, rows], pi[m, rows]
                obr = a * gr + b * gi
                obi = a * gi - b * gr
                sum_r = obr if sum_r is None else sum_r + obr
                sum_i = obi if sum_i is None else sum_i + obi
                pg[0, m, rows] += u * gr + v * gi
                pg[1, m, rows] += u * gi - v * gr
            og_r[rows] = sum_r
            og_i[rows] = sum_i
        low = lane < sh
        for part, src in ((0, og_r), (1, og_i)):
            for c in range(0, SIZE, CHUNK):
                a = pltpu.roll(src[c : c + CHUNK, :half], sh, 1)
                b = pltpu.roll(src[c : c + CHUNK, half:], sh, 1)
                acc[part, jb, pl.ds(y + c, CHUNK), :] += jnp.where(low, 0.0, a)
                acc[part, jb + 1, pl.ds(y + c, CHUNK), :] += jnp.where(low, a, b)
                acc[part, jb + 2, pl.ds(y + c, CHUNK), :] += jnp.where(low, b, 0.0)
        return carry

    lax.fori_loop(0, cnt[0, 0], frame, 0)


def combine_kernel(
    rows,
    cols,
    acc,
    pg,
    below,
    side,
    result,
    band,
    corner,
    data,
    rbuf0,
    rbuf1,
    rbuf2,
    local_sem,
    halo_send,
    halo_recv,
    sum_send,
    sum_recv,
):
    row, col = grid_place()
    n = 4
    core, x = lax.rem(col, 2), col // 2
    z, y = lax.rem(row, n), row // n
    up = (lax.rem(row + rows - 1, rows), col)
    down = (lax.rem(row + 1, rows), col)
    left = (row, lax.rem(col + cols - 1, cols))
    right = (row, lax.rem(col + 1, cols))
    other = (row, x * 2 + 1 - core)

    def at_place(dx, dy, dz):
        return (
            lax.rem(y + dy, n) * n + lax.rem(z + dz, n),
            lax.rem(x + dx, n) * 2 + core,
        )

    steps = [(a, b) for a in range(n) for b in range(n) if a or b]
    lines = ([at_place(0, k, 0) for k in (1, 2, 3)], [at_place(k, 0, 0) for k in (1, 2, 3)])
    planes = ([at_place(a, 0, b) for a, b in steps], [at_place(0, a, b) for a, b in steps])
    line_at = (y, x)
    plane_at = (x, y)

    loads = [
        pltpu.make_async_copy(pg, data, local_sem.at[0]),
        pltpu.make_async_copy(
            acc.at[:, pl.ds(0, 2), pl.ds(TILE, SIZE), :], band, local_sem.at[1]
        ),
    ]
    for copy in loads:
        copy.start()
    greet(
        [up, down, left, right, other]
        + planes[0]
        + [p for p, (a, b) in zip(planes[1], steps) if a]
    )

    def halo(src, dst, number, device):
        return pltpu.make_async_remote_copy(
            src_ref=src,
            dst_ref=dst,
            send_sem=halo_send.at[number],
            recv_sem=halo_recv.at[number],
            device_id=device,
            device_id_type=MESH,
        )

    corner_copy = halo(acc.at[:, pl.ds(4, 2), pl.ds(TILE, SIZE), :], corner, 0, right)
    has_up, has_down, has_left, has_right = row > 0, row < rows - 1, col > 0, col < cols - 1
    moves = {"corner": corner_copy}
    for part in range(2):
        moves["far", part] = halo(
            acc.at[part, pl.ds(2, 2), pl.ds(TILE, SIZE), :], below.at[part, pl.ds(2, 2)], 1 + part, down
        )
        moves["near", part] = halo(band.at[part], below.at[part, pl.ds(0, 2)], 3 + part, down)
        moves["side", part] = halo(
            acc.at[part, pl.ds(4, 2), pl.ds(0, TILE), :], side.at[part], 5 + part, right
        )

    def begin(stage):
        for name in SCHEDULE[stage]:

            @pl.when(has_right if name == "corner" or name[0] == "side" else has_down)
            def _():
                moves[name].start()

    begin(0)

    numbers = iter(range(82))
    pending = []

    def send(src, dst, device):
        number = next(numbers)
        copy = pltpu.make_async_remote_copy(
            src_ref=src,
            dst_ref=dst,
            send_sem=sum_send.at[number],
            recv_sem=sum_recv.at[number],
            device_id=device,
            device_id_type=MESH,
        )
        copy.start()
        pending.append(copy)
        return copy

    def aligned(start, size):
        return pl.ds(pl.multiple_of(start, 8), size)

    whole = 2 * MODES * SIZE
    kept = whole // 2
    part_rows = kept // 2
    quarter = part_rows // n
    piece = quarter // (n * n)
    mine = core * kept
    theirs = (1 - core) * kept
    loads[0].wait()
    core_copies = [
        send(
            data.at[aligned(theirs + part * part_rows, part_rows), :],
            rbuf0.at[pl.ds(part * part_rows, part_rows), :],
            other,
        )
        for part in range(2)
    ]

    begin(1)
    line_copies = []
    for part in range(2):
        core_copies[part].wait_recv()
        base = mine + part * part_rows

        def add_core(i, carry, base=base, part=part):
            here = aligned(base + i * quarter, quarter)
            data[here, :] += rbuf0[pl.ds(pl.multiple_of(part * part_rows + i * quarter, 8), quarter), :]
            return carry

        lax.fori_loop(0, n, add_core, 0)
        for k in (1, 2, 3):
            q = lax.rem(line_at[part] + k, n)
            line_copies.append(
                send(
                    data.at[aligned(base + q * quarter, quarter), :],
                    rbuf1.at[pl.ds((part * 3 + k - 1) * quarter, quarter), :],
                    lines[part][k - 1],
                )
            )

    loads[1].wait()

    @pl.when(has_left)
    def _():
        corner_copy.wait_recv()
        for part in range(2):
            for j in range(2):
                band[part, j] += corner[part, j]

    begin(2)

    bases = []
    plane_copies = []
    for part in range(2):
        for k in range(3):
            line_copies[part * 3 + k].wait_recv()
        base = mine + part * part_rows + line_at[part] * quarter
        bases.append(base)
        here = aligned(base, quarter)
        total = data[here, :]
        for k in range(3):
            total += rbuf1[(part * 3 + k) * quarter : (part * 3 + k + 1) * quarter, :]
        data[here, :] = total
        for k, (a, b) in enumerate(steps):
            q = lax.rem(plane_at[part] + a, n) * n + lax.rem(z + b, n)
            plane_copies.append(
                send(
                    data.at[aligned(base + q * piece, piece), :],
                    rbuf2.at[pl.ds((part * 15 + k) * piece, piece), :],
                    planes[part][k],
                )
            )
    begin(3)

    gather_copies = []
    for part in range(2):
        for k in range(15):
            plane_copies[part * 15 + k].wait_recv()
        here = aligned(bases[part] + (plane_at[part] * n + z) * piece, piece)
        total = data[here, :]
        for k in range(15):
            total += rbuf2[(part * 15 + k) * piece : (part * 15 + k + 1) * piece, :]
        result[here, :] = total
        for k in range(15):
            gather_copies.append(
                send(result.at[here, :], result.at[here, :], planes[part][k])
            )

    begin(4)
    line_copies = []
    for part in range(2):
        for k in range(15):
            gather_copies[part * 15 + k].wait_recv()
        here = result.at[aligned(bases[part], quarter), :]
        for k in (1, 2, 3):
            line_copies.append(send(here, here, lines[part][k - 1]))
    core_copies = []
    for part in range(2):
        here = result.at[aligned(bases[part], quarter), :]
        core_copies.append(send(here, here, other))
    begin(5)
    for k in (1, 3, 2):
        for part in range(2):
            line_copies[part * 3 + k - 1].wait_recv()
            q = lax.rem(line_at[part] + n - k, n)
            here = result.at[aligned(mine + part * part_rows + q * quarter, quarter), :]
            core_copies.append(send(here, here, other))
    for copy in core_copies:
        copy.wait_recv()
    for copy in pending:
        copy.wait_send()
    for name, copy in moves.items():
        sideways = name == "corner" or name[0] == "side"
        if name != "corner":
            pl.when(has_left if sideways else has_up)(copy.wait_recv)
        pl.when(has_right if sideways else has_down)(copy.wait_send)


def finish_kernel(step, acc, below, side, result, obj_r, obj_i, pr, pi, new_r, new_i, new_pr, new_pi):
    row, col = grid_place()
    upper = (pl.program_id(0) < 2) & (row > 0)
    for part, obj, new in ((0, obj_r, new_r), (1, obj_i, new_i)):
        for j in range(4):
            lanes = slice(j * LANES, (j + 1) * LANES)
            total = acc[part, j] + jnp.where(upper, below[part, j], 0.0)
            if j < 2:
                total += jnp.where(col > 0, side[part, j], 0.0)
            new[:, lanes] = obj[:, lanes] - OBJECT_STEP * total
    for part, old, new in ((0, pr, new_pr), (1, pi, new_pi)):
        new[0] = old[0] - step * result[part, 0]


def shards(object_real, object_imag, probe_real, probe_imag, amplitudes, positions, counts):
    rows, cols = lax.axis_size("row"), lax.axis_size("col")
    vmem = pl.BlockSpec(memory_space=pltpu.VMEM)
    smem = pl.BlockSpec(memory_space=pltpu.SMEM)
    anywhere = pl.BlockSpec(memory_space=pl.ANY)
    dma = pltpu.SemaphoreType.DMA
    extended = jax.ShapeDtypeStruct((2, 6, SPAN, LANES), F32)
    frame_shape = (SIZE, SIZE)

    mail = pl.pallas_call(
        lambda *refs: halo_kernel(rows, cols, *refs),
        out_shape=jax.ShapeDtypeStruct((BLOCKS, SIZE, LANES), F32),
        in_specs=[anywhere] * 3,
        out_specs=anywhere,
        scratch_shapes=[
            pltpu.VMEM((SLOTS, SIZE, SIZE), F32),
            pltpu.VMEM((2 * SLOTS, SIZE, LANES), F32),
            pltpu.VMEM((2, SIZE, SIZE), BF16),
            dma((SLOTS,)),
            dma,
            dma((20,)),
            dma((20,)),
        ],
        compiler_params=pltpu.CompilerParams(
            collective_id=0, has_side_effects=True, vmem_limit_bytes=HALO_LIMIT
        ),
        name="halo",
    )(object_real, object_imag, amplitudes[0, 0])

    acc, pg = pl.pallas_call(
        frames_kernel,
        out_shape=(extended, jax.ShapeDtypeStruct((2, MODES, SIZE, SIZE), F32)),
        in_specs=[smem, smem] + [anywhere] * 3 + [vmem] * 2 + [anywhere],
        out_specs=(vmem, vmem),
        scratch_shapes=[
            pltpu.VMEM((4, SIZE, SIZE), BF16),
            pltpu.VMEM((2 * SLOTS, SIZE, LANES), F32),
            pltpu.VMEM((2, 6, SPAN, LANES), F32),
            pltpu.VMEM(frame_shape, F32),
            pltpu.VMEM(frame_shape, F32),
            pltpu.VMEM((MODES, SIZE, SIZE), BF16),
            pltpu.VMEM((MODES, SIZE, SIZE), BF16),
            pltpu.VMEM((MODES * SIZE, SIZE), BF16),
            pltpu.VMEM((MODES * SIZE, SIZE), BF16),
            pltpu.VMEM((MODES, SIZE, SIZE), F32),
            pltpu.VMEM((MODES, SIZE, SIZE), F32),
            pltpu.VMEM(frame_shape, F32),
            pltpu.VMEM(frame_shape, F32),
            pltpu.VMEM(frame_shape, F32),
            dma((24,)),
        ],
        compiler_params=pltpu.CompilerParams(vmem_limit_bytes=28 * 2**20),
        name="frames",
    )(
        positions,
        counts,
        object_real,
        object_imag,
        mail,
        probe_real,
        probe_imag,
        jnp.asarray(tables()),
    )

    step = PROBE_STEP / math.sqrt(SLOTS * rows * cols)
    tile_shape = jax.ShapeDtypeStruct((TILE, TILE), F32)
    probe_shape = jax.ShapeDtypeStruct((MODES, SIZE, SIZE), F32)
    whole = 2 * MODES * SIZE
    below, side, result = pl.pallas_call(
        lambda *refs: combine_kernel(rows, cols, *refs),
        out_shape=(
            jax.ShapeDtypeStruct((2, 4, SIZE, LANES), F32),
            jax.ShapeDtypeStruct((2, 2, TILE, LANES), F32),
            jax.ShapeDtypeStruct((whole, SIZE), F32),
        ),
        in_specs=[anywhere, anywhere],
        out_specs=(anywhere, anywhere, vmem),
        scratch_shapes=[
            pltpu.VMEM((2, 2, SIZE, LANES), F32),
            pltpu.VMEM((2, 2, SIZE, LANES), F32),
            pltpu.VMEM((whole, SIZE), F32),
            pltpu.VMEM((whole // 2, SIZE), F32),
            pltpu.VMEM((whole // 2 * 3 // 4, SIZE), F32),
            pltpu.VMEM((30 * whole // 256, SIZE), F32),
            dma((2,)),
            dma((7,)),
            dma((7,)),
            dma((82,)),
            dma((82,)),
        ],
        compiler_params=pltpu.CompilerParams(
            collective_id=1, has_side_effects=True, vmem_limit_bytes=16 * 2**20
        ),
        name="combine",
    )(acc, pg.reshape(whole, SIZE))

    part = TILE // 4
    tile_block = pl.BlockSpec((part, TILE), lambda i: (i, 0))
    probe_block = pl.BlockSpec((1, SIZE, SIZE), lambda i: (i, 0, 0))
    return pl.pallas_call(
        lambda *refs: finish_kernel(step, *refs),
        grid=(4,),
        out_shape=(tile_shape, tile_shape, probe_shape, probe_shape),
        in_specs=[
            pl.BlockSpec((2, 4, part, LANES), lambda i: (0, 0, i, 0)),
            pl.BlockSpec((2, 4, part, LANES), lambda i: (0, 0, jnp.minimum(i, 1), 0)),
            pl.BlockSpec((2, 2, part, LANES), lambda i: (0, 0, i, 0)),
            pl.BlockSpec((2, 1, SIZE, SIZE), lambda i: (0, i, 0, 0)),
            tile_block,
            tile_block,
            probe_block,
            probe_block,
        ],
        out_specs=(tile_block, tile_block, probe_block, probe_block),
        compiler_params=pltpu.CompilerParams(vmem_limit_bytes=16 * 2**20),
        name="finish",
    )(
        acc,
        below,
        side,
        result.reshape(2, MODES, SIZE, SIZE),
        object_real,
        object_imag,
        probe_real,
        probe_imag,
    )


def solution(mesh):
    in_specs = (
        P("row", "col"),
        P("row", "col"),
        P(),
        P(),
        P("row", "col", None, None, None),
        P("row", "col", None, None),
        P("row", "col"),
    )
    out_specs = (P("row", "col"), P("row", "col"), P(), P())
    return jax.shard_map(shards, mesh=mesh, in_specs=in_specs, out_specs=out_specs, check_vma=False)
```

```python
import math

import jax
import jax.numpy as jnp
import numpy as np
from jax import lax
from jax.experimental import pallas as pl
from jax.experimental.pallas import tpu as pltpu
from jax.sharding import PartitionSpec as P

OBJECT_STEP = 0.25
PROBE_STEP = 0.5
MESH = pl.DeviceIdType.MESH
F32 = jnp.float32
BF16 = jnp.bfloat16
LANES = 128
SIZE = 256
MODES = 4
TILE = 512
SPAN = TILE + SIZE
SLOTS = 8
OWN_ROWS = MODES * SIZE
CHUNK = 32
HALO_LIMIT = 56 * 2**20
LOWER = 0
WIDE = 8
AMPS = 20
RELAY = 40
BLOCKS = 288
DETOUR = 128
HOP_ROWS = 64
EARLY_SIDES = 8
BAND_STEP = 0
SIDE_STEP = 0
CORNER_STEP = 1
SCHEDULE = (
    ("corner", ("far", 0)),
    (),
    (("far", 1),),
    (("side", 0), ("side", 1)),
    (("near", 0),),
    (("near", 1),),
)


def tables():
    index = np.arange(SIZE)
    angle = (index[:, None] * index[None, :] % SIZE) * (2.0 * math.pi / SIZE)
    scale = 1.0 / math.sqrt(SIZE)
    cos_t = (np.cos(angle) * scale).astype(BF16)
    sin_t = (-np.sin(angle) * scale).astype(BF16)
    found = []
    for parity in range(2):
        c = cos_t[parity::2, : SIZE // 2]
        s = sin_t[parity::2, : SIZE // 2]
        table = np.block([[c, -s], [s, c]])
        found += [table, np.ascontiguousarray(table.T)]
    return np.stack(found)


def dot(a, b):
    return jnp.dot(a, b, preferred_element_type=F32)


def grid_place():
    return lax.axis_index("row"), lax.axis_index("col")


def greet(peers):
    barrier = pltpu.get_barrier_semaphore()
    for peer in peers:
        pl.semaphore_signal(barrier, inc=1, device_id=peer, device_id_type=MESH)
    pl.semaphore_wait(barrier, len(peers))


def halo_kernel(
    rows, cols, obj_r, obj_i, amp_in, mail, amp, sorted_amp, order, load_sem, store_sem, send_sem, recv_sem
):
    row, col = grid_place()
    up = (lax.rem(row + rows - 1, rows), col)
    down = (lax.rem(row + 1, rows), col)
    left = (row, lax.rem(col + cols - 1, cols))
    right = (row, lax.rem(col + 1, cols))
    loads = [pltpu.make_async_copy(amp_in.at[s], amp.at[s], load_sem.at[s]) for s in range(SLOTS)]
    for copy in loads:
        copy.start()
    n = 4
    z, y = lax.rem(row, n), row // n
    following = (y * n + lax.rem(z + 1, n), col)
    previous = (y * n + lax.rem(z + n - 1, n), col)
    y_up = (lax.rem(y + n - 1, n) * n + z, col)
    y_down = (lax.rem(y + 1, n) * n + z, col)
    greet((up, down, left, right, following, previous, y_up, y_down))
    objs = (obj_r, obj_i)
    has_up, has_down, has_left, has_right = row > 0, row < rows - 1, col > 0, col < cols - 1

    def band(part, j, number):
        taken = SIZE if j < 3 else SIZE - DETOUR
        return pltpu.make_async_remote_copy(
            src_ref=objs[part].at[pl.ds(0, taken), pl.ds(j * LANES, LANES)],
            dst_ref=mail.at[LOWER + part * 4 + j, pl.ds(0, taken), :],
            send_sem=send_sem.at[number],
            recv_sem=recv_sem.at[number],
            device_id=up,
            device_id_type=MESH,
        )

    def side(part, j, third, number):
        return pltpu.make_async_remote_copy(
            src_ref=objs[part].at[pl.ds(third * SIZE, SIZE), pl.ds(j * LANES, LANES)],
            dst_ref=mail.at[WIDE + (part * 2 + j) * 3 + third],
            send_sem=send_sem.at[number],
            recv_sem=recv_sem.at[number],
            device_id=left,
            device_id_type=MESH,
        )

    def corner(part, j, number):
        return pltpu.make_async_remote_copy(
            src_ref=mail.at[LOWER + part * 4 + j],
            dst_ref=mail.at[WIDE + (part * 2 + j) * 3 + 2],
            send_sem=send_sem.at[number],
            recv_sem=recv_sem.at[number],
            device_id=left,
            device_id_type=MESH,
        )

    bands = [band(part, j, 2 * j + part) for j in range(4) for part in range(2)]
    sides = [
        side(part, j, third, 8 + 4 * third + 2 * j + part)
        for third in range(2)
        for j in range(2)
        for part in range(2)
    ]
    corners = [corner(part, j, 16 + 2 * j + part) for j in range(2) for part in range(2)]

    def hop(number, chunk, part):
        rows_here = pl.ds(SIZE - DETOUR + chunk * HOP_ROWS, HOP_ROWS)
        place = 20 + (number * (DETOUR // HOP_ROWS) + chunk) * 2 + part
        if number == 0:
            src = objs[part].at[rows_here, pl.ds(3 * LANES, LANES)]
        else:
            src = mail.at[RELAY + 2 * (number - 1) + part, rows_here, :]
        return pltpu.make_async_remote_copy(
            src_ref=src,
            dst_ref=mail.at[RELAY + 2 * number + part, rows_here, :],
            send_sem=send_sem.at[place],
            recv_sem=recv_sem.at[place],
            device_id=following if number < 3 else y_up,
            device_id_type=MESH,
        )

    chunks = DETOUR // HOP_ROWS
    hops = [[[hop(k, c, part) for part in range(2)] for c in range(chunks)] for k in range(4)]
    for c in range(chunks):
        for copy in hops[0][c]:
            copy.start()
    gives, takes = (z == n - 1) & (y > 0), (z == n - 1) & (y < n - 1)

    def start_bands(group):
        @pl.when(has_up)
        def _():
            for copy in group:
                copy.start()

    def start_sides(group):
        @pl.when(has_left)
        def _():
            for copy in group:
                copy.start()

    start_bands(bands[:4])
    start_sides(sides[:EARLY_SIDES])

    half = SIZE // 2
    first = lax.broadcasted_iota(jnp.int32, (SIZE, SIZE), 0)
    second = lax.broadcasted_iota(jnp.int32, (SIZE, SIZE), 1)

    def source(i):
        return jnp.where(i < half, 2 * i, 2 * (i - half) + 1)

    order[0] = jnp.where(first == source(second), 1.0, 0.0).astype(BF16)
    order[1] = jnp.where(second == source(first), 1.0, 0.0).astype(BF16)
    for copy in loads:
        copy.wait()

    def sort(slot, carry):
        a = amp[slot]
        by_row = jnp.zeros((SIZE, SIZE), F32)
        for step in range(3):
            piece = a.astype(BF16)
            by_row += dot(order[1], piece)
            a = a - piece.astype(F32)
        total = jnp.zeros((SIZE, SIZE), F32)
        for step in range(3):
            piece = by_row.astype(BF16)
            total += dot(piece, order[0])
            by_row = by_row - piece.astype(F32)
        sorted_amp[2 * slot] = total[:, :half]
        sorted_amp[2 * slot + 1] = total[:, half:]
        return carry

    lax.fori_loop(0, SLOTS, sort, 0)
    store = pltpu.make_async_copy(sorted_amp, mail.at[pl.ds(AMPS, 2 * SLOTS)], store_sem)
    store.start()

    def start_corners():
        for number in range(4):

            @pl.when(has_down)
            def _():
                bands[number].wait_recv()

            @pl.when(has_down & has_left)
            def _():
                corners[number].start()

    for step in range(chunks + 2):
        for k in (2, 1, 0):
            c = step - k
            if 0 <= c < chunks:
                for part in range(2):
                    hops[k][c][part].wait_recv()
                    if k < 2:
                        hops[k + 1][c][part].start()
                    else:
                        pl.when(gives)(hops[3][c][part].start)
        if step == BAND_STEP:
            start_bands(bands[4:])
        if step == SIDE_STEP:
            start_sides(sides[EARLY_SIDES:])
        if step == CORNER_STEP:
            start_corners()

    @pl.when(has_down)
    def _():
        for copy in bands[4:]:
            copy.wait_recv()

    @pl.when(has_up)
    def _():
        for copy in bands:
            copy.wait_send()

    @pl.when(has_right)
    def _():
        for copy in sides:
            copy.wait_recv()

    @pl.when(has_left)
    def _():
        for copy in sides:
            copy.wait_send()

    @pl.when(has_down & has_right)
    def _():
        for copy in corners:
            copy.wait_recv()

    @pl.when(has_down & has_left)
    def _():
        for copy in corners:
            copy.wait_send()

    for c in range(chunks):
        for part in range(2):
            for k in range(3):
                hops[k][c][part].wait_send()
            pl.when(gives)(hops[3][c][part].wait_send)
            pl.when(takes)(hops[3][c][part].wait_recv)
    store.wait()


def frames_kernel(
    pos,
    cnt,
    obj_r,
    obj_i,
    mail,
    pr,
    pi,
    tab_in,
    acc,
    pg,
    tab,
    amp,
    ext,
    pat_r,
    pat_i,
    xp,
    xq,
    xe,
    xo,
    far_e,
    far_o,
    inten,
    og_r,
    og_i,
    sem,
):
    row, col = grid_place()
    arrived = jnp.where(lax.rem(row, 4) == 3, 2, 0)
    half = SIZE // 2
    loads = [
        pltpu.make_async_copy(
            mail.at[pl.ds(LOWER + 4 * part, 3)],
            ext.at[part, pl.ds(0, 3), pl.ds(TILE, SIZE), :],
            sem.at[part],
        )
        for part in range(2)
    ] + [
        pltpu.make_async_copy(
            mail.at[LOWER + 4 * part + 3, pl.ds(0, SIZE - DETOUR), :],
            ext.at[part, 3, pl.ds(TILE, SIZE - DETOUR), :],
            sem.at[24 + part],
        )
        for part in range(2)
    ] + [
        pltpu.make_async_copy(
            mail.at[RELAY + 4 + arrived + part, pl.ds(SIZE - DETOUR, DETOUR), :],
            ext.at[part, 3, pl.ds(TILE + SIZE - DETOUR, DETOUR), :],
            sem.at[26 + part],
        )
        for part in range(2)
    ] + [
        pltpu.make_async_copy(
            mail.at[WIDE + (part * 2 + j) * 3 + third],
            ext.at[part, 4 + j, pl.ds(third * SIZE, SIZE), :],
            sem.at[12 + (part * 2 + j) * 3 + third],
        )
        for part in range(2)
        for j in range(2)
        for third in range(3)
    ]
    loads.append(pltpu.make_async_copy(mail.at[pl.ds(AMPS, 2 * SLOTS)], amp, sem.at[11]))
    loads.append(pltpu.make_async_copy(tab_in, tab, sem.at[10]))
    for copy in loads:
        copy.start()
    for part, obj in ((0, obj_r), (1, obj_i)):
        for j in range(4):
            ext[part, j, :TILE] = obj[:, j * LANES : (j + 1) * LANES]
    blank = jnp.zeros((SPAN, LANES), F32)
    for part in range(2):
        for j in range(6):
            acc[part, j] = blank
        for m in range(MODES):
            pg[part, m] = jnp.zeros((SIZE, SIZE), F32)
    for copy in loads:
        copy.wait()

    def frame(s, carry):
        y = pos[0, 0, s, 0]
        x = pos[0, 0, s, 1]
        jb = x // LANES
        sh = x % LANES
        back = (LANES - sh) % LANES
        lane = lax.broadcasted_iota(jnp.int32, (CHUNK, LANES), 1)
        keep = lane < LANES - sh
        for part, dst in ((0, pat_r), (1, pat_i)):
            for c in range(0, SIZE, CHUNK):
                a, b, d = (
                    pltpu.roll(ext[part, jb + t, pl.ds(y + c, CHUNK), :], back, 1) for t in range(3)
                )
                dst[c : c + CHUNK, :half] = jnp.where(keep, a, b)
                dst[c : c + CHUNK, half:] = jnp.where(keep, b, d)
        for m in range(MODES):
            for c in range(0, half, CHUNK):
                w = []
                for o in (c, c + half):
                    a, b = pr[m, o : o + CHUNK], pi[m, o : o + CHUNK]
                    u, v = pat_r[o : o + CHUNK], pat_i[o : o + CHUNK]
                    w.append((a * u - b * v, a * v + b * u))
                (tr, ti), (br, bi) = w
                xp[m, c : c + CHUNK] = (tr + br).astype(BF16)
                xp[m, c + half : c + half + CHUNK] = (ti + bi).astype(BF16)
                xq[m, c : c + CHUNK] = (tr - br).astype(BF16)
                xq[m, c + half : c + half + CHUNK] = (ti - bi).astype(BF16)
        for m in range(MODES):
            for p, src in ((0, xp), (1, xq)):
                h = dot(tab[2 * p], src[m])
                rows = slice(m * SIZE + p * half, m * SIZE + (p + 1) * half)
                for part in range(2):
                    first, second = h[part * half : (part + 1) * half, :half], h[part * half : (part + 1) * half, half:]
                    lanes = slice(part * half, (part + 1) * half)
                    xe[rows, lanes] = (first + second).astype(BF16)
                    xo[rows, lanes] = (first - second).astype(BF16)
        far_e[...] = dot(xe[...], tab[1]).reshape(MODES, SIZE, SIZE)
        far_o[...] = dot(xo[...], tab[3]).reshape(MODES, SIZE, SIZE)
        for c in range(0, SIZE, CHUNK):
            rows = slice(c, c + CHUNK)
            for side, far in enumerate((far_e, far_o)):
                total = None
                for m in range(MODES):
                    f = far[m, rows]
                    f = f * f
                    f = f[:, :half] + f[:, half:]
                    total = f if total is None else total + f
                inten[rows, side * half : (side + 1) * half] = 1.0 - amp[2 * s + side, rows] * lax.rsqrt(
                    jnp.maximum(total, 0.25)
                )
        for m in range(MODES):
            for p, dst in ((0, xp), (1, xq)):
                for c in range(0, half, CHUNK):
                    rows = slice(p * half + c, p * half + c + CHUNK)
                    f0, f1 = inten[rows, :half], inten[rows, half:]
                    e, o = far_e[m, rows], far_o[m, rows]
                    dst[m, c : c + CHUNK] = jnp.concatenate(
                        [e[:, :half] * f0, o[:, :half] * f1], axis=1
                    ).astype(BF16)
                    dst[m, c + half : c + half + CHUNK] = jnp.concatenate(
                        [e[:, half:] * f0, o[:, half:] * f1], axis=1
                    ).astype(BF16)
        for m in range(MODES):
            a = dot(tab[1], xp[m])
            b = dot(tab[3], xq[m])
            for p, v in ((0, a + b), (1, a - b)):
                v = v.astype(BF16)
                rows = slice(m * SIZE + p * half, m * SIZE + (p + 1) * half)
                xe[rows, :half] = v[:half, :half]
                xe[rows, half:] = v[half:, :half]
                xo[rows, :half] = v[:half, half:]
                xo[rows, half:] = v[half:, half:]
        far_e[...] = dot(xe[...], tab[0]).reshape(MODES, SIZE, SIZE)
        far_o[...] = dot(xo[...], tab[2]).reshape(MODES, SIZE, SIZE)
        for c in range(0, SIZE, CHUNK):
            rows = slice(c, c + CHUNK)
            u, v = pat_r[rows], pat_i[rows]
            sum_r = sum_i = None
            for m in range(MODES):
                ga, gb = far_e[m, rows], far_o[m, rows]
                sm, df = ga + gb, ga - gb
                gr = jnp.concatenate([sm[:, :half], df[:, :half]], axis=1)
                gi = jnp.concatenate([sm[:, half:], df[:, half:]], axis=1)
                a, b = pr[m, rows], pi[m, rows]
                obr = a * gr + b * gi
                obi = a * gi - b * gr
                sum_r = obr if sum_r is None else sum_r + obr
                sum_i = obi if sum_i is None else sum_i + obi
                pg[0, m, rows] += u * gr + v * gi
                pg[1, m, rows] += u * gi - v * gr
            og_r[rows] = sum_r
            og_i[rows] = sum_i
        low = lane < sh
        for part, src in ((0, og_r), (1, og_i)):
            for c in range(0, SIZE, CHUNK):
                a = pltpu.roll(src[c : c + CHUNK, :half], sh, 1)
                b = pltpu.roll(src[c : c + CHUNK, half:], sh, 1)
                acc[part, jb, pl.ds(y + c, CHUNK), :] += jnp.where(low, 0.0, a)
                acc[part, jb + 1, pl.ds(y + c, CHUNK), :] += jnp.where(low, a, b)
                acc[part, jb + 2, pl.ds(y + c, CHUNK), :] += jnp.where(low, b, 0.0)
        return carry

    lax.fori_loop(0, cnt[0, 0], frame, 0)


def combine_kernel(
    rows,
    cols,
    acc,
    pg,
    below,
    side,
    result,
    band,
    corner,
    data,
    rbuf0,
    rbuf1,
    rbuf2,
    local_sem,
    halo_send,
    halo_recv,
    sum_send,
    sum_recv,
):
    row, col = grid_place()
    n = 4
    core, x = lax.rem(col, 2), col // 2
    z, y = lax.rem(row, n), row // n
    up = (lax.rem(row + rows - 1, rows), col)
    down = (lax.rem(row + 1, rows), col)
    left = (row, lax.rem(col + cols - 1, cols))
    right = (row, lax.rem(col + 1, cols))
    other = (row, x * 2 + 1 - core)

    def at_place(dx, dy, dz):
        return (
            lax.rem(y + dy, n) * n + lax.rem(z + dz, n),
            lax.rem(x + dx, n) * 2 + core,
        )

    steps = [(a, b) for a in range(n) for b in range(n) if a or b]
    lines = ([at_place(0, k, 0) for k in (1, 2, 3)], [at_place(k, 0, 0) for k in (1, 2, 3)])
    planes = ([at_place(a, 0, b) for a, b in steps], [at_place(0, a, b) for a, b in steps])
    line_at = (y, x)
    plane_at = (x, y)

    loads = [
        pltpu.make_async_copy(
            pg.at[pl.ds(pl.multiple_of(core * OWN_ROWS, OWN_ROWS), OWN_ROWS), :], data, local_sem.at[0]
        ),
        pltpu.make_async_copy(
            acc.at[:, pl.ds(0, 2), pl.ds(TILE, SIZE), :], band, local_sem.at[1]
        ),
    ]
    for copy in loads:
        copy.start()
    greet(
        [up, down, left, right, other]
        + planes[0]
        + [p for p, (a, b) in zip(planes[1], steps) if a]
    )

    def halo(src, dst, number, device):
        return pltpu.make_async_remote_copy(
            src_ref=src,
            dst_ref=dst,
            send_sem=halo_send.at[number],
            recv_sem=halo_recv.at[number],
            device_id=device,
            device_id_type=MESH,
        )

    corner_copy = halo(acc.at[:, pl.ds(4, 2), pl.ds(TILE, SIZE), :], corner, 0, right)
    has_up, has_down, has_left, has_right = row > 0, row < rows - 1, col > 0, col < cols - 1
    moves = {"corner": corner_copy}
    for part in range(2):
        moves["far", part] = halo(
            acc.at[part, pl.ds(2, 2), pl.ds(TILE, SIZE), :], below.at[part, pl.ds(2, 2)], 1 + part, down
        )
        moves["near", part] = halo(band.at[part], below.at[part, pl.ds(0, 2)], 3 + part, down)
        moves["side", part] = halo(
            acc.at[part, pl.ds(4, 2), pl.ds(0, TILE), :], side.at[part], 5 + part, right
        )

    def begin(stage):
        for name in SCHEDULE[stage]:

            @pl.when(has_right if name == "corner" or name[0] == "side" else has_down)
            def _():
                moves[name].start()

    numbers = iter(range(82))
    pending = []

    def send(src, dst, device):
        number = next(numbers)
        copy = pltpu.make_async_remote_copy(
            src_ref=src,
            dst_ref=dst,
            send_sem=sum_send.at[number],
            recv_sem=sum_recv.at[number],
            device_id=device,
            device_id_type=MESH,
        )
        copy.start()
        pending.append(copy)
        return copy

    def aligned(start, size):
        return pl.ds(pl.multiple_of(start, 8), size)

    whole = 2 * MODES * SIZE
    kept = whole // 2
    part_rows = kept // 2
    quarter = part_rows // n
    piece = quarter // (n * n)
    mine = core * kept
    theirs = (1 - core) * kept
    core_copies = [
        send(
            pg.at[aligned(theirs + part * part_rows, part_rows), :],
            rbuf0.at[pl.ds(part * part_rows, part_rows), :],
            other,
        )
        for part in range(2)
    ]

    begin(0)
    begin(1)
    loads[0].wait()
    line_copies = []
    for part in range(2):
        core_copies[part].wait_recv()
        base = part * part_rows

        def add_core(i, carry, base=base, part=part):
            here = aligned(base + i * quarter, quarter)
            data[here, :] += rbuf0[pl.ds(pl.multiple_of(part * part_rows + i * quarter, 8), quarter), :]
            return carry

        lax.fori_loop(0, n, add_core, 0)
        for k in (1, 2, 3):
            q = lax.rem(line_at[part] + k, n)
            line_copies.append(
                send(
                    data.at[aligned(base + q * quarter, quarter), :],
                    rbuf1.at[pl.ds((part * 3 + k - 1) * quarter, quarter), :],
                    lines[part][k - 1],
                )
            )

    loads[1].wait()

    @pl.when(has_left)
    def _():
        corner_copy.wait_recv()
        for part in range(2):
            for j in range(2):
                band[part, j] += corner[part, j]

    begin(2)

    bases = []
    plane_copies = []
    for part in range(2):
        for k in range(3):
            line_copies[part * 3 + k].wait_recv()
        base = part * part_rows + line_at[part] * quarter
        bases.append(base)
        here = aligned(base, quarter)
        total = data[here, :]
        for k in range(3):
            total += rbuf1[(part * 3 + k) * quarter : (part * 3 + k + 1) * quarter, :]
        data[here, :] = total
        for k, (a, b) in enumerate(steps):
            q = lax.rem(plane_at[part] + a, n) * n + lax.rem(z + b, n)
            plane_copies.append(
                send(
                    data.at[aligned(base + q * piece, piece), :],
                    rbuf2.at[pl.ds((part * 15 + k) * piece, piece), :],
                    planes[part][k],
                )
            )
    begin(3)

    gather_copies = []
    for part in range(2):
        for k in range(15):
            plane_copies[part * 15 + k].wait_recv()
        offset = bases[part] + (plane_at[part] * n + z) * piece
        total = data[aligned(offset, piece), :]
        here = aligned(mine + offset, piece)
        for k in range(15):
            total += rbuf2[(part * 15 + k) * piece : (part * 15 + k + 1) * piece, :]
        result[here, :] = total
        for k in range(15):
            gather_copies.append(
                send(result.at[here, :], result.at[here, :], planes[part][k])
            )

    begin(4)
    line_copies = []
    for part in range(2):
        for k in range(15):
            gather_copies[part * 15 + k].wait_recv()
        here = result.at[aligned(mine + bases[part], quarter), :]
        for k in (1, 2, 3):
            line_copies.append(send(here, here, lines[part][k - 1]))
    core_copies = []
    for part in range(2):
        here = result.at[aligned(mine + bases[part], quarter), :]
        core_copies.append(send(here, here, other))
    begin(5)
    for k in (1, 3, 2):
        for part in range(2):
            line_copies[part * 3 + k - 1].wait_recv()
            q = lax.rem(line_at[part] + n - k, n)
            here = result.at[aligned(mine + part * part_rows + q * quarter, quarter), :]
            core_copies.append(send(here, here, other))
    for copy in core_copies:
        copy.wait_recv()
    for copy in pending:
        copy.wait_send()
    for name, copy in moves.items():
        sideways = name == "corner" or name[0] == "side"
        if name != "corner":
            pl.when(has_left if sideways else has_up)(copy.wait_recv)
        pl.when(has_right if sideways else has_down)(copy.wait_send)


def finish_kernel(step, acc, below, side, result, obj_r, obj_i, pr, pi, new_r, new_i, new_pr, new_pi):
    row, col = grid_place()
    upper = (pl.program_id(0) < 1) & (row > 0)
    for part, obj, new in ((0, obj_r, new_r), (1, obj_i, new_i)):
        for j in range(4):
            lanes = slice(j * LANES, (j + 1) * LANES)
            total = acc[part, j] + jnp.where(upper, below[part, j], 0.0)
            if j < 2:
                total += jnp.where(col > 0, side[part, j], 0.0)
            new[:, lanes] = obj[:, lanes] - OBJECT_STEP * total
    for part, old, new in ((0, pr, new_pr), (1, pi, new_pi)):
        new[...] = old[...] - step * result[part]


def shards(object_real, object_imag, probe_real, probe_imag, amplitudes, positions, counts):
    rows, cols = lax.axis_size("row"), lax.axis_size("col")
    vmem = pl.BlockSpec(memory_space=pltpu.VMEM)
    smem = pl.BlockSpec(memory_space=pltpu.SMEM)
    anywhere = pl.BlockSpec(memory_space=pl.ANY)
    dma = pltpu.SemaphoreType.DMA
    extended = jax.ShapeDtypeStruct((2, 6, SPAN, LANES), F32)
    frame_shape = (SIZE, SIZE)

    mail = pl.pallas_call(
        lambda *refs: halo_kernel(rows, cols, *refs),
        out_shape=jax.ShapeDtypeStruct((BLOCKS, SIZE, LANES), F32),
        in_specs=[anywhere] * 3,
        out_specs=anywhere,
        scratch_shapes=[
            pltpu.VMEM((SLOTS, SIZE, SIZE), F32),
            pltpu.VMEM((2 * SLOTS, SIZE, LANES), F32),
            pltpu.VMEM((2, SIZE, SIZE), BF16),
            dma((SLOTS,)),
            dma,
            dma((20 + 8 * (DETOUR // HOP_ROWS),)),
            dma((20 + 8 * (DETOUR // HOP_ROWS),)),
        ],
        compiler_params=pltpu.CompilerParams(
            collective_id=0, has_side_effects=True, vmem_limit_bytes=HALO_LIMIT
        ),
        name="halo",
    )(object_real, object_imag, amplitudes[0, 0])

    acc, pg = pl.pallas_call(
        frames_kernel,
        out_shape=(extended, jax.ShapeDtypeStruct((2, MODES, SIZE, SIZE), F32)),
        in_specs=[smem, smem] + [vmem] * 2 + [anywhere] + [vmem] * 2 + [anywhere],
        out_specs=(vmem, vmem),
        scratch_shapes=[
            pltpu.VMEM((4, SIZE, SIZE), BF16),
            pltpu.VMEM((2 * SLOTS, SIZE, LANES), F32),
            pltpu.VMEM((2, 6, SPAN, LANES), F32),
            pltpu.VMEM(frame_shape, F32),
            pltpu.VMEM(frame_shape, F32),
            pltpu.VMEM((MODES, SIZE, SIZE), BF16),
            pltpu.VMEM((MODES, SIZE, SIZE), BF16),
            pltpu.VMEM((MODES * SIZE, SIZE), BF16),
            pltpu.VMEM((MODES * SIZE, SIZE), BF16),
            pltpu.VMEM((MODES, SIZE, SIZE), F32),
            pltpu.VMEM((MODES, SIZE, SIZE), F32),
            pltpu.VMEM(frame_shape, F32),
            pltpu.VMEM(frame_shape, F32),
            pltpu.VMEM(frame_shape, F32),
            dma((28,)),
        ],
        compiler_params=pltpu.CompilerParams(vmem_limit_bytes=28 * 2**20),
        name="frames",
    )(
        positions,
        counts,
        object_real,
        object_imag,
        mail,
        probe_real,
        probe_imag,
        jnp.asarray(tables()),
    )

    step = PROBE_STEP / math.sqrt(SLOTS * rows * cols)
    tile_shape = jax.ShapeDtypeStruct((TILE, TILE), F32)
    probe_shape = jax.ShapeDtypeStruct((MODES, SIZE, SIZE), F32)
    whole = 2 * MODES * SIZE
    below, side, result = pl.pallas_call(
        lambda *refs: combine_kernel(rows, cols, *refs),
        out_shape=(
            jax.ShapeDtypeStruct((2, 4, SIZE, LANES), F32),
            jax.ShapeDtypeStruct((2, 2, TILE, LANES), F32),
            jax.ShapeDtypeStruct((whole, SIZE), F32),
        ),
        in_specs=[anywhere, anywhere],
        out_specs=(anywhere, anywhere, vmem),
        scratch_shapes=[
            pltpu.VMEM((2, 2, SIZE, LANES), F32),
            pltpu.VMEM((2, 2, SIZE, LANES), F32),
            pltpu.VMEM((whole // 2, SIZE), F32),
            pltpu.VMEM((whole // 2, SIZE), F32),
            pltpu.VMEM((whole // 2 * 3 // 4, SIZE), F32),
            pltpu.VMEM((30 * whole // 256, SIZE), F32),
            dma((2,)),
            dma((7,)),
            dma((7,)),
            dma((82,)),
            dma((82,)),
        ],
        compiler_params=pltpu.CompilerParams(
            collective_id=1, has_side_effects=True, vmem_limit_bytes=16 * 2**20
        ),
        name="combine",
    )(acc, pg.reshape(whole, SIZE))

    part = TILE // 2
    tile_block = pl.BlockSpec((part, TILE), lambda i: (i, 0))
    probe_block = pl.BlockSpec((2, SIZE, SIZE), lambda i: (i, 0, 0))
    return pl.pallas_call(
        lambda *refs: finish_kernel(step, *refs),
        grid=(2,),
        out_shape=(tile_shape, tile_shape, probe_shape, probe_shape),
        in_specs=[
            pl.BlockSpec((2, 4, part, LANES), lambda i: (0, 0, i, 0)),
            pl.BlockSpec((2, 4, SIZE, LANES), lambda i: (0, 0, 0, 0)),
            pl.BlockSpec((2, 2, part, LANES), lambda i: (0, 0, i, 0)),
            pl.BlockSpec((2, 2, SIZE, SIZE), lambda i: (0, i, 0, 0)),
            tile_block,
            tile_block,
            probe_block,
            probe_block,
        ],
        out_specs=(tile_block, tile_block, probe_block, probe_block),
        compiler_params=pltpu.CompilerParams(vmem_limit_bytes=16 * 2**20),
        name="finish",
    )(
        acc,
        below,
        side,
        result.reshape(2, MODES, SIZE, SIZE),
        object_real,
        object_imag,
        probe_real,
        probe_imag,
    )


def solution(mesh):
    in_specs = (
        P("row", "col"),
        P("row", "col"),
        P(),
        P(),
        P("row", "col", None, None, None),
        P("row", "col", None, None),
        P("row", "col"),
    )
    out_specs = (P("row", "col"), P("row", "col"), P(), P())
    return jax.shard_map(shards, mesh=mesh, in_specs=in_specs, out_specs=out_specs, check_vma=False)
```
